32 devices in a mesh: dp: 16 (over z, y, core), mp: 2 (over x).
Axes of the slice: x: 2, y: 2, z: 4, core: 2. Of those that a mesh axis runs over, the one named last changes fastest.
Arguments:
- tokens: bfloat16 [32768, 1024], P(('dp', 'mp')), may hold values from -6 to 6
- cotangent: bfloat16 [32768, 1024], P(('dp', 'mp')), may hold values from -18 to 18
- lengths: int32 [16, 8], P('dp'), may hold values from 1 to 1280, 2048 in all within a row
- pad_count: int32 [16], P('dp'), may hold values from 0 to 256
- ln1_gain: float32 [1024], replicated, may hold values from 0.5 to 1.5
- ln1_bias: float32 [1024], replicated, may hold values from -4 to 4
- ln2_gain: float32 [1024], replicated, may hold values from 0.5 to 1.5
- ln2_bias: float32 [1024], replicated, may hold values from -4 to 4
- qkv_weight: bfloat16 [1024, 3, 1024], P(None, None, 'mp'), may hold values from -0.1875 to 0.1875
- qkv_bias: float32 [3, 1024], P(None, 'mp'), may hold values from -6 to 6
- out_weight: bfloat16 [1024, 1024], P('mp'), may hold values from -1 to 1
- out_bias: float32 [1024], replicated, may hold values from -6 to 6
- fc1_weight: bfloat16 [1024, 4096], P(None, 'mp'), may hold values from -0.1875 to 0.1875
- fc1_bias: float32 [4096], P('mp'), may hold values from -6 to 6
- fc2_weight: bfloat16 [4096, 1024], P('mp'), may hold values from -0.09375 to 0.09375
Outputs:
- output: bfloat16 [32768, 1024], P(('dp', 'mp'))
- grad_tokens: float32 [32768, 1024], P(('dp', 'mp'))
- grad_ln1_gain: float32 [1024], replicated
- grad_ln1_bias: float32 [1024], replicated
- grad_ln2_gain: float32 [1024], replicated
- grad_ln2_bias: float32 [1024], replicated
- grad_qkv_weight: float32 [1024, 3, 1024], P(None, None, 'mp')
- grad_qkv_bias: float32 [3, 1024], P(None, 'mp')
- grad_out_weight: float32 [1024, 1024], P('mp')
- grad_out_bias: float32 [1024], replicated
- grad_fc1_weight: float32 [1024, 4096], P(None, 'mp')
- grad_fc1_bias: float32 [4096], P('mp')
- grad_fc2_weight: float32 [4096, 1024], P('mp')
The draws below stay inside these ranges and needn't reach their ends.
Inputs may be any that keep to these rules, and one draw needn't show every extreme that they name: Each row lists its 8 document lengths in order; they sum to 2048 and the largest is exactly 1280.
All inputs are finite; a program needn't handle non-finite values.
Results may differ from the reference program's by a relative error of at most 0.012.
Values may be sent and summed in bfloat16 or wider, within the bound.
No kernel may reach another device: no remote copies, remote signals or barrier semaphores. Data moves between devices by JAX's collectives and lax.ppermute only.
A program may use at most 448 MiB of HBM per device.

```python
import math
from functools import partial
import jax
import jax.numpy as jnp
import numpy as np
from jax import lax

D = 1024
HEADS = 16
HEAD = 64
ROT = 16
FF = 4096
ROW_LEN = 2048
DOCS = 8
MOST = 1280
PAD_MAX = 256
ROWS = 16
TOKENS = 32768


def draw_cotangent(key, part):
    key = jax.random.fold_in(key, 11)
    row_total = TOKENS // ROW_LEN
    row_of = jnp.arange(TOKENS, dtype=jnp.int32) // ROW_LEN
    scaling = 1.0 + 2.0 * row_of.astype(jnp.float32) / max(row_total - 1, 1)
    base = jax.random.truncated_normal(key, -6.0, 6.0, (TOKENS, D), jnp.float32)
    return (base * scaling[:, None]).astype(jnp.bfloat16)


def set_ends(values, own_key, low, high):
    longest = values.shape.index(max(values.shape))
    spots = []
    for shift in (0, 1):
        where = [jax.random.randint(jax.random.fold_in(own_key, axis), (), 0, length) for axis, length in enumerate(values.shape)]
        where[longest] = (where[longest] + shift) % values.shape[longest]
        spots.append(tuple(where))
    return values.at[spots[0]].set(low).at[spots[1]].set(high)


def shard_levels(stream_key, shape, cuts, least, high):
    level, own = 1.0, jax.random.fold_in(stream_key, 6)
    for dim, shards_of in cuts:
        heights = jnp.exp(jax.random.uniform(jax.random.fold_in(own, dim), (shards_of,), jnp.float32, least / len(cuts), high / len(cuts)))
        level = level * jnp.repeat(heights, shape[dim] // shards_of).reshape([-1 if axis == dim else 1 for axis in range(len(shape))])
    return level


def length_profile(amount, total, limit, skew):
    portions = [(1 << 20) // math.isqrt(standing ** skew) + 1 for standing in range(2, amount + 1)]
    surplus, counts = total - limit - (amount - 1), [1] * (amount - 1)
    while surplus > 0:
        free = [i for i in range(amount - 1) if counts[i] < limit]
        pool, budget = sum([portions[i] for i in free]), surplus
        for i in free:
            more = min(limit - counts[i], max(1, budget * portions[i] // pool), surplus)
            counts[i] = counts[i] + more
            surplus = surplus - more
    return np.array([limit] + counts)


def uneven(key, amount, total, bound, skew):
    if amount == 2:
        one = jax.random.randint(key, (), max(1, total - bound), min(bound, total - 1) + 1)
        return jnp.stack([one, total - one])
    sizes = jnp.asarray(length_profile(amount, total, bound, skew), jnp.int32)
    pairs = (amount - 1) // 2
    source_of, receiver = sizes[1:1 + 2 * pairs:2], sizes[2:2 + 2 * pairs:2]
    slack = jnp.minimum(source_of - 1, bound - receiver)
    passed = jax.random.randint(jax.random.fold_in(key, 1), (pairs,), 0, 1 << 20) % (slack + 1)
    sizes = sizes.at[1:1 + 2 * pairs:2].set(source_of - passed).at[2:2 + 2 * pairs:2].set(receiver + passed)
    return sizes[jax.random.permutation(jax.random.fold_in(key, 2), amount)]


def bell_draw(stream_key, dims, width, bound, split=(), kind=jnp.bfloat16):
    level = shard_levels(stream_key, dims, split, -0.22, 0.18) if split else 1.0
    array = jax.random.normal(stream_key, dims, jnp.float32) * width * level
    return jnp.minimum(jnp.maximum(array, -bound), bound).astype(kind)


def setup_inputs(seed: int = 0) -> dict:
    key_of = jax.random.split(jax.random.key(seed), 16)
    return {
        "tokens": bell_draw(key_of[0], (TOKENS, D), 1.0, 6.0, ((0, 32),)),
        "cotangent": draw_cotangent(jax.random.fold_in(key_of[15], 71), 0),
        "lengths": jax.vmap(lambda own: uneven(own, DOCS, ROW_LEN, MOST, 2))(jax.random.split(key_of[2], ROWS)).reshape((ROWS, DOCS)).astype(jnp.int32),
        "pad_count": set_ends(jax.random.randint(key_of[3], (ROWS,), 0, PAD_MAX + 1), jax.random.fold_in(key_of[3], 1), 0, PAD_MAX).astype(jnp.int32),
        "ln1_gain": jnp.clip(1.0 + 0.1 * jax.random.normal(key_of[4], (D,), jnp.float32), 0.5, 1.5),
        "ln1_bias": bell_draw(key_of[5], (D,), 0.3, 4.0, (), jnp.float32),
        "ln2_gain": jnp.clip(1.0 + 0.1 * jax.random.normal(key_of[6], (D,), jnp.float32), 0.5, 1.5),
        "ln2_bias": bell_draw(key_of[7], (D,), 0.3, 4.0, (), jnp.float32),
        "qkv_weight": bell_draw(key_of[8], (D, 3, D), D ** -0.5, 0.1875, ((2, 2),)),
        "qkv_bias": bell_draw(key_of[9], (3, D), 0.5, 6.0, ((1, 2),), jnp.float32),
        "out_weight": bell_draw(key_of[10], (D, D), (D // 32) ** -0.5, 1.0, ((0, 2),)),
        "out_bias": bell_draw(key_of[11], (D,), 0.5, 6.0, (), jnp.float32),
        "fc1_weight": bell_draw(key_of[12], (D, FF), D ** -0.5, 0.1875, ((1, 2),)),
        "fc1_bias": bell_draw(key_of[13], (FF,), 0.5, 6.0, ((0, 2),), jnp.float32),
        "fc2_weight": bell_draw(key_of[14], (FF, D), FF ** -0.5, 0.09375, ((0, 2),)),
    }


@jax.custom_vjp
def low(v):
    return lax.optimization_barrier(v.astype(jnp.bfloat16)).astype(jnp.float32)

@jax.custom_vjp
def low_back(v):
    return v

def low_keep(v):
    return (low(v), None)

def low_pass(kept, grad):
    return (grad,)

def back_keep(v):
    return (v, None)

def back_low(kept, grad):
    return (low(grad),)
low.defvjp(low_keep, low_pass)
low_back.defvjp(back_keep, back_low)
EPSILON = 1e-05
MASKED_SCORE = -1e+30
ROTARY_BASE = 10000.0

def layer_norm(v, gain, shift):
    average = lax.optimization_barrier(jnp.mean(v, axis=-1, keepdims=True))
    centred = v - average
    spread = lax.optimization_barrier(jnp.mean(centred * centred, axis=-1, keepdims=True))
    return centred * lax.rsqrt(spread + EPSILON) * gain + shift

def row_layout(row_lengths, pad_tokens, row_len):
    doc_ends = jnp.cumsum(row_lengths).astype(jnp.int32)
    doc_starts = doc_ends - row_lengths
    places = jnp.arange(row_len, dtype=jnp.int32)
    segment = lax.optimization_barrier(jnp.sum((places[:, None] >= doc_ends[None, :]).astype(jnp.int32), axis=1))
    owners = segment[:, None] == jnp.arange(row_lengths.shape[0], dtype=jnp.int32)[None, :]
    doc_start = lax.optimization_barrier(jnp.sum(jnp.where(owners, doc_starts[None, :], 0), axis=1)).astype(jnp.int32)
    position = places - doc_start
    keep_mask = places < row_len - pad_tokens
    return (segment, position, keep_mask)

def rotary(v, position):
    half_rot = ROT // 2
    frequency = ROTARY_BASE ** (-(jnp.arange(half_rot, dtype=jnp.float32) * 2.0) / ROT)
    angles = position.astype(jnp.float32)[:, None] * frequency[None, :]
    cosine = jnp.concatenate([jnp.cos(angles), jnp.cos(angles)], axis=1)[:, None, :]
    sine_table = jnp.concatenate([jnp.sin(angles), jnp.sin(angles)], axis=1)[:, None, :]
    turned = v[..., :ROT]
    front_half = turned[..., :half_rot]
    back_half = turned[..., half_rot:]
    rolled = jnp.concatenate([-back_half, front_half], axis=-1)
    return jnp.concatenate([turned * cosine + rolled * sine_table, v[..., ROT:]], axis=-1)

def allowed_pairs(seg_rows, keep_rows, place_rows, seg_cols, keep_cols, place_cols):
    joined = (seg_rows[:, None] == seg_cols[None, :]) & keep_rows[:, None] & keep_cols[None, :]
    joined = joined & (place_cols[None, :] <= place_rows[:, None])
    return joined | (place_cols[None, :] == place_rows[:, None])

def block_forward(inputs, parameters, segment, position, keep_mask, block_rows):
    gain1, shift1, gain2, shift2, w_qkv, b_qkv, w_out, b_out, w_fc1, b_fc1, w_fc2 = parameters
    highest = lax.Precision.HIGHEST
    normed1 = low(layer_norm(inputs, gain1, shift1))
    normed2 = low(layer_norm(inputs, gain2, shift2))
    projected = low_back(jnp.einsum('td,dce->cte', normed1, w_qkv, precision=highest) + b_qkv[:, None, :])
    queries = low(rotary(projected[0].reshape(ROW_LEN, HEADS, HEAD), position))
    key_rot = low(rotary(projected[1].reshape(ROW_LEN, HEADS, HEAD), position))
    values = low(projected[2].reshape(ROW_LEN, HEADS, HEAD))
    places = jnp.arange(ROW_LEN, dtype=jnp.int32)
    scaling = HEAD ** (-0.5)

    def attend(index):
        offset = (index * block_rows).astype(jnp.int32)
        query_part = lax.dynamic_slice_in_dim(queries, offset, block_rows, 0)
        seg_part = lax.dynamic_slice_in_dim(segment, offset, block_rows, 0)
        keep_part = lax.dynamic_slice_in_dim(keep_mask, offset, block_rows, 0)
        place_part = lax.dynamic_slice_in_dim(places, offset, block_rows, 0)
        scores = low_back(jnp.einsum('qhd,khd->hqk', query_part, key_rot, precision=highest) * scaling)
        masked = jnp.where(allowed_pairs(seg_part, keep_part, place_part, segment, keep_mask, places)[None], scores, MASKED_SCORE)
        largest = lax.optimization_barrier(jnp.max(masked, axis=-1, keepdims=True))
        expo = jnp.exp(masked - largest)
        probs = expo / lax.optimization_barrier(jnp.sum(expo, axis=-1, keepdims=True))
        return jnp.einsum('hqk,khd->qhd', low(probs), values, precision=highest)
    pieces = lax.map(jax.checkpoint(attend), jnp.arange(ROW_LEN // block_rows, dtype=jnp.int32))
    attended = low(low_back(pieces.reshape(ROW_LEN, D)))
    attn_part = jnp.dot(attended, w_out, precision=highest)
    pre_act = low_back(jnp.dot(normed2, w_fc1, precision=highest) + b_fc1)
    activated = low(jax.nn.gelu(pre_act, approximate=False))
    mlp_part = jnp.dot(activated, w_fc2, precision=highest)
    return inputs + attn_part + mlp_part + b_out

def reference(tokens, cotangent, lengths, pad_count, ln1_gain, ln1_bias, ln2_gain, ln2_bias, qkv_weight, qkv_bias, out_weight, out_bias, fc1_weight, fc1_bias, fc2_weight):
    parameters = (ln1_gain, ln1_bias, ln2_gain, ln2_bias, qkv_weight.astype(jnp.float32), qkv_bias, out_weight.astype(jnp.float32), out_bias, fc1_weight.astype(jnp.float32), fc1_bias, fc2_weight.astype(jnp.float32))
    block_rows = min(512, ROW_LEN)
    rows_in = tokens.astype(jnp.float32).reshape(ROWS, ROW_LEN, D)
    rows_ct = cotangent.astype(jnp.float32).reshape(ROWS, ROW_LEN, D)

    def one_row(carry, row_item):
        inputs, row_ct, row_lengths, pad_tokens = row_item
        segment, position, keep_mask = row_layout(row_lengths, pad_tokens, ROW_LEN)
        forward = partial(block_forward, segment=segment, position=position, keep_mask=keep_mask, block_rows=block_rows)
        result, pullback = jax.vjp(forward, inputs, parameters)
        grad_inputs, grad_parameters = pullback(row_ct * keep_mask.astype(jnp.float32)[:, None])
        carry = jax.tree.map(lambda a, b: a + b, carry, grad_parameters)
        return (carry, (result.astype(jnp.bfloat16), grad_inputs))
    zeros = jax.tree.map(jnp.zeros_like, parameters)
    totals, (outputs, grad_rows) = lax.scan(one_row, zeros, (rows_in, rows_ct, lengths, pad_count))
    return (outputs.reshape(TOKENS, D), grad_rows.reshape(TOKENS, D), totals[0], totals[1], totals[2], totals[3], totals[4], totals[5], totals[6], totals[7], totals[8], totals[9], totals[10])
```

```python
import functools

import jax
import jax.numpy as jnp
from jax import lax
from jax.experimental import pallas as pl
from jax.experimental.pallas import tpu as pltpu
from jax.sharding import PartitionSpec as P

HEAD = 64
ROT = 16
PAIR = 2 * HEAD
EPSILON = 1e-05
MASKED_SCORE = -1e30
ROTARY_BASE = 10000.0
SCALING = HEAD**-0.5
F32 = jnp.float32
BF16 = jnp.bfloat16
NN = ((1,), (0,))
NT = ((1,), (1,))
TN = ((0,), (0,))
MIB = 2**20


def dot(a, b, dims=NN):
    return lax.dot_general(a, b, (dims, ((), ())), preferred_element_type=F32)


def norm_stats(v):
    average = jnp.mean(v, axis=-1, keepdims=True)
    centred = v - average
    spread = jnp.mean(centred * centred, axis=-1, keepdims=True)
    return centred, lax.rsqrt(spread + EPSILON)


def turn(x, cosine, sine):
    half = ROT // 2
    u, w = x[:half], x[half:ROT]
    return jnp.concatenate([u * cosine - w * sine, w * cosine + u * sine, x[ROT:]], axis=0)


def project_body(place_ref, tok_ref, g_ref, gain_ref, shift_ref, w_ref, b_ref, wo_ref, cos_ref, sin_ref, *rest):
    q_out, kt_out, vt_out, k_out, v_out, n_out, do_out = rest[-7:]
    x = tok_ref[...].astype(F32)
    centred, rstd = norm_stats(x)
    normed = (centred * rstd * gain_ref[...] + shift_ref[...]).astype(BF16)
    n_out[...] = normed
    cosine, sine = cos_ref[...], sin_ref[...]
    width = wo_ref.shape[0]

    def head_rows(c, scale):
        p = dot(w_ref[c * width : (c + 1) * width, :], normed, NT) + b_ref[c * width : (c + 1) * width, :]
        if c == 2:
            return p.astype(BF16)
        parts = [turn(p[h : h + HEAD], cosine, sine) for h in range(0, width, HEAD)]
        return (jnp.concatenate(parts, axis=0) * scale).astype(BF16)

    q_out[...] = head_rows(0, SCALING)
    k = head_rows(1, 1.0)
    kt_out[...] = k
    k_out[...] = k.T
    v = head_rows(2, 1.0)
    vt_out[...] = v
    v_out[...] = v.T
    do_out[...] = dot(wo_ref[...], g_ref[...], NT).astype(BF16)


def project(place, tok, g, gain, shift, w_t, b_col, w_out, cosine, sine, row_len, before):
    half, d = tok.shape
    width = w_out.shape[0]
    rows = 256
    steps = half // rows
    here = lambda i, place: (i, 0)
    lanes = lambda i, place: (0, place[0] * steps + i)
    seq = lambda i, place: (place[0] * steps + i, 0)
    fixed = lambda i, place: (0, 0)
    specs = [
        pl.BlockSpec((rows, d), here),
        pl.BlockSpec((rows, d), here),
        pl.BlockSpec((1, d), fixed),
        pl.BlockSpec((1, d), fixed),
        pl.BlockSpec((3 * width, d), fixed),
        pl.BlockSpec((3 * width, 1), fixed),
        pl.BlockSpec((width, d), fixed),
        pl.BlockSpec((ROT // 2, rows), lanes),
        pl.BlockSpec((ROT // 2, rows), lanes),
    ]
    args = [place, tok, g, gain, shift, w_t, b_col, w_out, cosine, sine]
    aliases = {}
    if before is not None:
        specs += [pl.BlockSpec(memory_space=pl.ANY)] * 6
        aliases = {len(args) + i: i for i in range(6)}
        args += list(before)
    wide = jax.ShapeDtypeStruct((width, row_len), BF16)
    tall = jax.ShapeDtypeStruct((row_len, width), BF16)
    return pl.pallas_call(
        project_body,
        grid_spec=pltpu.PrefetchScalarGridSpec(
            num_scalar_prefetch=1,
            grid=(steps,),
            in_specs=specs,
            out_specs=[pl.BlockSpec((width, rows), lanes)] * 3
            + [pl.BlockSpec((rows, width), seq)] * 2
            + [pl.BlockSpec((rows, d), seq)]
            + [pl.BlockSpec((width, rows), lambda i, place: (0, i))],
        ),
        out_shape=[wide, wide, wide, tall, tall, jax.ShapeDtypeStruct((row_len, d), BF16), jax.ShapeDtypeStruct((width, half), BF16)],
        input_output_aliases=aliases,
        compiler_params=pltpu.CompilerParams(vmem_limit_bytes=40 * MIB),
        cost_estimate=pl.CostEstimate(flops=8 * half * d * width, bytes_accessed=16 * MIB, transcendentals=0),
        name="project",
    )(*args)


def gelu_parts(v):
    t = 1.0 / (1.0 + (0.3275911 * 0.7071067811865476) * jnp.abs(v))
    bell = jnp.exp(-0.5 * (v * v))
    poly = t * (0.127414796 + t * (-0.142248368 + t * (0.7107068705 + t * (-0.7265760135 + t * 0.5307027145))))
    tail = poly * bell
    below = jnp.where(v < 0.0, tail, 1.0 - tail)
    return v * below, below + v * (bell * 0.3989422804014327)


def mlp_body(*refs, first, rows):
    tok_ref, g_ref, gain_ref, shift_ref, w1_ref, b1_ref, w2_ref = refs[:7]
    refs = refs[7:]
    if not first:
        dw1_in, dw2_in = refs[:2]
        refs = refs[2:]
    out_ref, e_ref, dw1_ref, dw2_ref, db1_ref, dgain_ref, dshift_ref = refs[:7]
    normed, normed_t, out_acc, back_acc, act_t, pre_t = refs[7:]
    step = pl.program_id(0)
    last = pl.num_programs(0) - 1
    half, d = normed.shape
    blocks = half // rows

    @pl.when(step == 0)
    def _():
        def prepare(i, _):
            at = pl.ds(pl.multiple_of(i * rows, rows), rows)
            centred, rstd = norm_stats(tok_ref[at, :].astype(F32))
            n = (centred * rstd * gain_ref[...] + shift_ref[...]).astype(BF16)
            normed[at, :] = n
            normed_t[:, at] = n.T
            return 0

        lax.fori_loop(0, blocks, prepare, 0)
        dgain_ref[...] = jnp.zeros_like(dgain_ref)
        dshift_ref[...] = jnp.zeros_like(dshift_ref)

    def forward(i, bias_sum):
        at = pl.ds(pl.multiple_of(i * rows, rows), rows)
        v = dot(normed[at, :], w1_ref[...]) + b1_ref[...]
        grad_act = dot(g_ref[at, :], w2_ref[...], NT)
        act, slope = gelu_parts(v)
        act = act.astype(BF16)
        grad_pre = (grad_act * slope).astype(BF16)
        out = dot(act, w2_ref[...])
        back = dot(grad_pre, w1_ref[...], NT)

        @pl.when(step == 0)
        def _():
            out_acc[at, :] = out
            back_acc[at, :] = back

        @pl.when(step > 0)
        def _():
            out_acc[at, :] += out
            back_acc[at, :] += back

        act_t[:, at] = act.T
        pre_t[at, :] = grad_pre
        return bias_sum + jnp.sum(grad_pre.astype(F32), axis=0, keepdims=True)

    db1_ref[...] = lax.fori_loop(0, blocks, forward, jnp.zeros(db1_ref.shape, F32))

    def weights(i, _):
        at = pl.ds(pl.multiple_of(i * rows, rows), rows)
        one = dot(normed_t[at, :], pre_t[...])
        if not first:
            one = one + dw1_in[at, :].astype(F32)
        dw1_ref[at, :] = one.astype(BF16)
        two = dot(act_t[...], g_ref[:, at])
        if not first:
            two = two + dw2_in[:, at].astype(F32)
        dw2_ref[:, at] = two.astype(BF16)
        return 0

    for i in range(d // rows):
        weights(i, 0)

    @pl.when(step == last)
    def _():
        def finish(i, _):
            at = pl.ds(pl.multiple_of(i * rows, rows), rows)
            centred, rstd = norm_stats(tok_ref[at, :].astype(F32))
            back = back_acc[at, :]
            dgain_ref[...] += jnp.sum(back * (centred * rstd), axis=0, keepdims=True)
            dshift_ref[...] += jnp.sum(back, axis=0, keepdims=True)
            e_ref[at, :] = (back * gain_ref[...]).astype(BF16)
            out_ref[at, :] = out_acc[at, :].astype(BF16)
            return 0

        lax.fori_loop(0, blocks, finish, 0)


def mlp(tok, g, gain, shift, w1, b1, w2, before):
    half, d = tok.shape
    hidden = w1.shape[1]
    chunk = 512
    rows = 256
    fixed = lambda j: (0, 0)
    cols = pl.BlockSpec((d, chunk), lambda j: (0, j))
    tall = pl.BlockSpec((chunk, d), lambda j: (j, 0))
    whole = pl.BlockSpec((half, d), fixed)
    line = pl.BlockSpec((1, d), fixed)
    bias = pl.BlockSpec((1, chunk), lambda j: (0, j))
    args = [tok, g, gain, shift, w1, b1, w2]
    specs = [whole, whole, line, line, cols, bias, tall]
    if before is not None:
        args += list(before)
        specs += [cols, tall]
    shape = jax.ShapeDtypeStruct
    return pl.pallas_call(
        functools.partial(mlp_body, first=before is None, rows=rows),
        grid=(hidden // chunk,),
        in_specs=specs,
        out_specs=[whole, whole, cols, tall, bias, line, line],
        out_shape=[
            shape((half, d), BF16),
            shape((half, d), BF16),
            shape((d, hidden), BF16),
            shape((hidden, d), BF16),
            shape((1, hidden), F32),
            shape((1, d), F32),
            shape((1, d), F32),
        ],
        scratch_shapes=[
            pltpu.VMEM((half, d), BF16),
            pltpu.VMEM((d, half), BF16),
            pltpu.VMEM((half, d), F32),
            pltpu.VMEM((half, d), F32),
            pltpu.VMEM((chunk, half), BF16),
            pltpu.VMEM((half, chunk), BF16),
        ],
        compiler_params=pltpu.CompilerParams(vmem_limit_bytes=56 * MIB),
        cost_estimate=pl.CostEstimate(flops=12 * half * d * hidden, bytes_accessed=32 * MIB, transcendentals=0),
        name="feed_forward",
    )(*args)


def fold(x, op):
    return op(x.reshape(x.shape[0] // 8, 8, x.shape[1]), axis=0)


def attention_body(info_ref, q_ref, kt, vt, do_ref, k_ref, v_ref, start_ref, cosq_ref, sinq_ref, *rest, first, block):
    if first:
        o_ref, dq_ref, dk_ref, dv_ref, s_scr, e_scr = rest
    else:
        cos_ref, sin_ref, dq_in, dk_in, dv_in, o_ref, grads_ref, s_scr, e_scr, dk_ref, dv_ref = rest
    step = pl.program_id(1)
    half = pl.num_programs(1) * block
    place = info_ref[0] * pl.num_programs(1) + step
    row_len = kt.shape[1]

    @pl.when(step == 0)
    def _():
        if first:
            dk_ref[...] = jnp.zeros_like(dk_ref)
            dv_ref[...] = jnp.zeros_like(dv_ref)
        else:
            dk_ref[...] = dk_in[...]
            dv_ref[...] = dv_in[...]

    q_t = q_ref[...]
    zeros = jnp.zeros((HEAD, block), BF16)
    q_wide = [jnp.concatenate([q_t[:HEAD], zeros], 0), jnp.concatenate([zeros, q_t[HEAD:]], 0)]
    start = start_ref[...]
    spot = place * block + lax.broadcasted_iota(jnp.int32, (1, block), 1)
    low = info_ref[1 + step]
    high = place + 1
    rows = lax.broadcasted_iota(jnp.int32, (block, block // 2), 0)

    def scores(kb, tops):
        tops = list(tops)
        off = pl.multiple_of(kb * block, block)
        k_blk = k_ref[pl.ds(off, block), :]
        for w in range(2):
            at = slice(w * block // 2, (w + 1) * block // 2)
            legal = (rows >= start[:, at] - off) & (rows <= spot[:, at] - off)
            for h in range(2):
                s = jnp.where(legal, dot(k_blk, q_wide[h][:, at]), MASKED_SCORE)
                s_scr[h, pl.ds(off, block), at] = s
                tops[2 * h + w] = jnp.maximum(tops[2 * h + w], fold(s, jnp.max))
        return tuple(tops)

    tops = lax.fori_loop(low, high, scores, (jnp.full((8, block // 2), MASKED_SCORE, F32),) * 4)
    top = [jnp.max(jnp.concatenate(tops[2 * h : 2 * h + 2], 1), axis=0, keepdims=True) for h in range(2)]

    def forward(kb, carry):
        carry = list(carry)
        off = pl.multiple_of(kb * block, block)
        for h in range(2):
            e = jnp.exp(s_scr[h, pl.ds(off, block), :] - top[h])
            carry[h] = carry[h] + fold(e, jnp.sum)
            e = e.astype(BF16)
            e_scr[h, pl.ds(off, block), :] = e
            carry[2 + h] = carry[2 + h] + dot(vt[h * HEAD : (h + 1) * HEAD, pl.ds(off, block)], e)
        return tuple(carry)

    eight, tall = jnp.zeros((8, block), F32), jnp.zeros((HEAD, block), F32)
    sums = lax.fori_loop(low, high, forward, (eight, eight, tall, tall))
    grad = do_ref[...].astype(F32)
    centre, grad_low, grad_wide = [], [], []
    for h in range(2):
        at = slice(h * HEAD, (h + 1) * HEAD)
        inverse = 1.0 / jnp.sum(sums[h], axis=0, keepdims=True)
        o = sums[2 + h] * inverse
        o_ref[at, :] = o.astype(BF16)
        scaled = grad[at] * inverse
        centre.append(jnp.sum(scaled * o, axis=0, keepdims=True))
        grad_low.append(scaled.astype(BF16))
    grad_wide = [jnp.concatenate([grad_low[0], zeros], 0), jnp.concatenate([zeros, grad_low[1]], 0)]

    def backward(kb, carry):
        carry = list(carry)
        off = pl.multiple_of(kb * block, block)
        here = pl.ds(off, block)
        v_blk = v_ref[here, :]
        for h in range(2):
            at = slice(h * HEAD, (h + 1) * HEAD)
            e = e_scr[h, here, :]
            ds = (e.astype(F32) * (dot(v_blk, grad_wide[h]) - centre[h])).astype(BF16)
            dv_ref[at, here] += dot(grad_low[h], e, NT)
            dk_ref[at, here] += dot(q_t[at], ds, NT)
            carry[h] = carry[h] + dot(kt[at, here], ds)
        return tuple(carry)

    grads = lax.fori_loop(low, high, backward, (tall, tall))
    turned = [turn(grads[h] * SCALING, cosq_ref[...], -sinq_ref[...]).astype(BF16) for h in range(2)]
    if first:
        dq_ref[...] = jnp.concatenate(turned, 0)
    else:
        off = pl.multiple_of(place * block, block)
        grads_ref[0, :, pl.ds(off, block)] = jnp.concatenate(turned, 0)

        @pl.when(step == pl.num_programs(1) - 1)
        def _():
            other = pl.multiple_of((1 - info_ref[0]) * half, half)
            grads_ref[0, :, pl.ds(other, half)] = dq_in[...]

            def finish(i, _):
                here = pl.ds(pl.multiple_of(i * block, block), block)
                cosine, sine = cos_ref[:, here], -sin_ref[:, here]
                for h in range(2):
                    at = slice(h * HEAD, (h + 1) * HEAD)
                    grads_ref[1, at, here] = turn(dk_ref[at, here], cosine, sine).astype(BF16)
                grads_ref[2, :, here] = dv_ref[:, here].astype(BF16)
                return 0

            lax.fori_loop(0, row_len // block, finish, 0)


def attention(info, q_t, k_t, v_t, do_t, k, v, start, cosine, sine, before):
    width, row_len = q_t.shape
    half = do_t.shape[1]
    block = 512
    steps = half // block
    first = before is None
    place = lambda p, i, info: (p, info[0] * steps + i)
    line = lambda p, i, info: (0, info[0] * steps + i)
    here = pl.BlockSpec((PAIR, block), lambda p, i, info: (p, i))
    wide = pl.BlockSpec((PAIR, row_len), lambda p, i, info: (p, 0))
    tall = pl.BlockSpec((row_len, PAIR), lambda p, i, info: (0, p))
    angle = pl.BlockSpec((ROT // 2, block), line)
    args = [info, q_t, k_t, v_t, do_t, k, v, start, cosine, sine]
    specs = [pl.BlockSpec((PAIR, block), place), wide, wide, here, tall, tall, pl.BlockSpec((1, block), line), angle, angle]
    shape = jax.ShapeDtypeStruct
    scratch = [pltpu.VMEM((2, row_len, block), F32), pltpu.VMEM((2, row_len, block), BF16)]
    if first:
        outs = [shape((width, half), BF16)] * 2 + [shape((width, row_len), F32)] * 2
        out_specs = [here, here, wide, wide]
    else:
        table = pl.BlockSpec((ROT // 2, row_len), lambda p, i, info: (0, 0))
        args += [cosine, sine, *before]
        specs += [table, table, pl.BlockSpec((PAIR, half), lambda p, i, info: (p, 0)), wide, wide]
        outs = [shape((width, half), BF16), shape((3, width, row_len), BF16)]
        out_specs = [here, pl.BlockSpec((3, PAIR, row_len), lambda p, i, info: (0, p, 0))]
        scratch += [pltpu.VMEM((PAIR, row_len), F32)] * 2
    return pl.pallas_call(
        functools.partial(attention_body, first=first, block=block),
        grid_spec=pltpu.PrefetchScalarGridSpec(
            num_scalar_prefetch=1,
            grid=(width // PAIR, steps),
            in_specs=specs,
            out_specs=out_specs,
            scratch_shapes=scratch,
        ),
        out_shape=outs,
        compiler_params=pltpu.CompilerParams(vmem_limit_bytes=48 * MIB),
        cost_estimate=pl.CostEstimate(flops=24 * half * half * width * 2, bytes_accessed=16 * MIB, transcendentals=0),
        name="attention",
    )(*args)


def per_device(
    tokens,
    cotangent,
    lengths,
    pad_count,
    ln1_gain,
    ln1_bias,
    ln2_gain,
    ln2_bias,
    qkv_weight,
    qkv_bias,
    out_weight,
    out_bias,
    fc1_weight,
    fc1_bias,
    fc2_weight,
):
    half, d = tokens.shape
    row_len = half * lax.axis_size("mp")
    width = qkv_weight.shape[2]
    me = lax.axis_index("mp")
    swap = [(0, 1), (1, 0)]
    tok_far = lax.ppermute(tokens, "mp", swap)
    cot_later, tok_far = lax.optimization_barrier((cotangent, tok_far))
    cot_far = lax.ppermute(cot_later, "mp", swap)

    docs = lengths.shape[1]
    order = jnp.arange(docs)
    starts = jnp.sum(jnp.where(order[None, :] < order[:, None], lengths[0][None, :], 0), axis=1)
    places = jnp.arange(row_len, dtype=jnp.int32)
    doc_start = jnp.max(jnp.where(starts[:, None] <= places[None, :], starts[:, None], 0), axis=0)
    kept = row_len - pad_count[0]
    start = jnp.where(places < kept, doc_start, places).astype(jnp.int32)
    frequency = ROTARY_BASE ** (-(jnp.arange(ROT // 2, dtype=F32) * 2.0) / ROT)
    angles = frequency[:, None] * (places - doc_start).astype(F32)[None, :]
    cosine, sine = jnp.cos(angles), jnp.sin(angles)
    block = 512
    lows = (start[::block] // block).astype(jnp.int32).reshape(2, -1)
    near = jnp.concatenate([me[None].astype(jnp.int32), lows[me]])
    far = jnp.concatenate([(1 - me)[None].astype(jnp.int32), lows[1 - me]])

    inside = jnp.arange(half, dtype=jnp.int32)[:, None]
    g_near = jnp.where(inside < kept - me * half, cotangent, jnp.zeros((), BF16))
    g_far = jnp.where(inside < kept - (1 - me) * half, cot_far, jnp.zeros((), BF16))

    gain1, shift1 = ln1_gain[None], ln1_bias[None]
    gain2, shift2 = ln2_gain[None], ln2_bias[None]
    w_t = jnp.transpose(qkv_weight, (1, 2, 0)).reshape(3 * width, d)
    b_col = qkv_bias.reshape(3 * width, 1)
    b1 = fc1_bias[None]

    mlp_near = mlp(tokens, g_near, gain2, shift2, fc1_weight, b1, fc2_weight, None)
    front = (gain1, shift1, w_t, b_col, out_weight, cosine, sine, row_len)
    *made, do_near = project(near[:1], tokens, g_near, *front, None)
    q_t, k_t, v_t, k, v, normed1, do_far = project(far[:1], tok_far, g_far, *front, made)
    o_near, dq_near, dk, dv = attention(near, q_t, k_t, v_t, do_near, k, v, start[None], cosine, sine, None)
    mlp_far = mlp(tok_far, g_far, gain2, shift2, fc1_weight, b1, fc2_weight, mlp_near[2:4])
    grad_fc1 = lax.psum(mlp_far[2], "dp")
    grad_fc2 = lax.psum(mlp_far[3], "dp")
    o_far, grads = attention(far, q_t, k_t, v_t, do_far, k, v, start[None], cosine, sine, (dq_near, dk, dv))

    branch_far = dot(o_far, out_weight, TN) + mlp_far[0].astype(F32)
    arrived = lax.ppermute(branch_far.astype(BF16), "mp", swap)
    branch = dot(o_near, out_weight, TN) + mlp_near[0].astype(F32)
    output = (tokens.astype(F32) + (branch + arrived.astype(F32)) + out_bias).astype(BF16)

    grads = grads.reshape(3 * width, row_len)
    grad_qkv = dot(grads, normed1).astype(BF16)
    grad_out_w = (dot(o_near, g_near) + dot(o_far, g_far)).astype(BF16)
    grad_qkv = lax.psum(grad_qkv, "dp")
    grad_out_w = lax.psum(grad_out_w, "dp")
    grad_qkv_b = jnp.sum(grads.astype(F32), axis=1)

    def norm_back(place, tok, e2):
        part = lax.dynamic_slice_in_dim(grads, place * half, half, 1)
        back = dot(part, w_t, TN)
        centred, rstd = norm_stats(tok.astype(F32))
        xhat = centred * rstd
        return gain1 * back + e2.astype(F32), jnp.sum(back * xhat, axis=0), jnp.sum(back, axis=0)

    e_far, dgain_far, dshift_far = norm_back(1 - me, tok_far, mlp_far[1])
    e_arrived = lax.ppermute(e_far.astype(BF16), "mp", swap)
    e_near, dgain_near, dshift_near = norm_back(me, tokens, mlp_near[1])
    e = e_near + e_arrived.astype(F32)
    centred, rstd = norm_stats(tokens.astype(F32))
    xhat = centred * rstd
    grad_in = rstd * (e - jnp.mean(e, axis=-1, keepdims=True) - xhat * jnp.mean(e * xhat, axis=-1, keepdims=True))
    g_wide = g_near.astype(F32)
    grad_tokens = g_wide + grad_in

    both = jnp.stack(
        [
            dgain_near + dgain_far,
            dshift_near + dshift_far,
            (mlp_near[5] + mlp_far[5])[0],
            (mlp_near[6] + mlp_far[6])[0],
            jnp.sum(g_wide, axis=0),
        ]
    )
    both = both + lax.ppermute(both, "mp", swap)
    small = jnp.concatenate([both.reshape(-1), grad_qkv_b, (mlp_near[4] + mlp_far[4])[0]])
    small = lax.psum(small, "dp")
    both = small[: 5 * d].reshape(5, d)
    grad_qkv_b = small[5 * d : 5 * d + 3 * width].reshape(3, width)
    grad_fc1_b = small[5 * d + 3 * width :]
    return (
        output,
        grad_tokens,
        both[0],
        both[1],
        both[2],
        both[3],
        jnp.transpose(grad_qkv.reshape(3, width, d), (2, 0, 1)).astype(F32),
        grad_qkv_b,
        grad_out_w.astype(F32),
        both[4],
        grad_fc1.astype(F32),
        grad_fc1_b,
        grad_fc2.astype(F32),
    )


def solution(mesh):
    return jax.shard_map(
        per_device,
        mesh=mesh,
        in_specs=(
            P(("dp", "mp"), None),
            P(("dp", "mp"), None),
            P("dp", None),
            P("dp"),
            P(),
            P(),
            P(),
            P(),
            P(None, None, "mp"),
            P(None, "mp"),
            P("mp", None),
            P(),
            P(None, "mp"),
            P("mp"),
            P("mp", None),
        ),
        out_specs=(
            P(("dp", "mp"), None),
            P(("dp", "mp"), None),
            P(),
            P(),
            P(),
            P(),
            P(None, None, "mp"),
            P(None, "mp"),
            P("mp", None),
            P(),
            P(None, "mp"),
            P("mp"),
            P("mp", None),
        ),
        check_vma=False,
    )
```

```python
import functools

import jax
import jax.numpy as jnp
from jax import lax
from jax.experimental import pallas as pl
from jax.experimental.pallas import tpu as pltpu
from jax.sharding import PartitionSpec as P

HEAD = 64
ROT = 16
PAIR = 2 * HEAD
EPSILON = 1e-05
MASKED_SCORE = -1e30
ROTARY_BASE = 10000.0
SCALING = HEAD**-0.5
F32 = jnp.float32
BF16 = jnp.bfloat16
NN = ((1,), (0,))
NT = ((1,), (1,))
TN = ((0,), (0,))
MIB = 2**20


def dot(a, b, dims=NN):
    return lax.dot_general(a, b, (dims, ((), ())), preferred_element_type=F32)


def cost(micros):
    return pl.CostEstimate(flops=int(micros * 1.1e9), bytes_accessed=0, transcendentals=0)


def norm_stats(v):
    average = jnp.mean(v, axis=-1, keepdims=True)
    centred = v - average
    spread = jnp.mean(centred * centred, axis=-1, keepdims=True)
    return centred, lax.rsqrt(spread + EPSILON)


def turn(x, cosine, sine):
    half = ROT // 2
    u, w = x[:half], x[half:ROT]
    return jnp.concatenate([u * cosine - w * sine, w * cosine + u * sine, x[ROT:]], axis=0)


def project_body(place_ref, tok_ref, gain_ref, shift_ref, w_ref, b_ref, cos_ref, sin_ref, *rest):
    q_out, kt_out, vt_out, k_out, v_out, n_out = rest[-6:]
    x = tok_ref[...].astype(F32)
    centred, rstd = norm_stats(x)
    normed = (centred * rstd * gain_ref[...] + shift_ref[...]).astype(BF16)
    n_out[...] = normed
    cosine, sine = cos_ref[...], sin_ref[...]
    width = k_out.shape[1]

    def head_rows(c, scale):
        p = dot(w_ref[c * width : (c + 1) * width, :], normed, NT) + b_ref[c * width : (c + 1) * width, :]
        if c == 2:
            return p.astype(BF16)
        parts = [turn(p[h : h + HEAD], cosine, sine) for h in range(0, width, HEAD)]
        return (jnp.concatenate(parts, axis=0) * scale).astype(BF16)

    q_out[...] = head_rows(0, SCALING)
    k = head_rows(1, 1.0)
    kt_out[...] = k
    k_out[...] = k.T
    v = head_rows(2, 1.0)
    vt_out[...] = v
    v_out[...] = v.T


def project(place, tok, gain, shift, w_t, b_col, cosine, sine, row_len, before):
    half, d = tok.shape
    width = w_t.shape[0] // 3
    rows = 256
    steps = half // rows
    here = lambda i, place: (i, 0)
    lanes = lambda i, place: (0, place[0] * steps + i)
    seq = lambda i, place: (place[0] * steps + i, 0)
    fixed = lambda i, place: (0, 0)
    specs = [
        pl.BlockSpec((rows, d), here),
        pl.BlockSpec((1, d), fixed),
        pl.BlockSpec((1, d), fixed),
        pl.BlockSpec((3 * width, d), fixed),
        pl.BlockSpec((3 * width, 1), fixed),
        pl.BlockSpec((ROT // 2, rows), lanes),
        pl.BlockSpec((ROT // 2, rows), lanes),
    ]
    args = [place, tok, gain, shift, w_t, b_col, cosine, sine]
    aliases = {}
    if before is not None:
        specs += [pl.BlockSpec(memory_space=pl.ANY)] * 6
        aliases = {len(args) + i: i for i in range(6)}
        args += list(before)
    wide = jax.ShapeDtypeStruct((width, row_len), BF16)
    tall = jax.ShapeDtypeStruct((row_len, width), BF16)
    return pl.pallas_call(
        project_body,
        grid_spec=pltpu.PrefetchScalarGridSpec(
            num_scalar_prefetch=1,
            grid=(steps,),
            in_specs=specs,
            out_specs=[pl.BlockSpec((width, rows), lanes)] * 3
            + [pl.BlockSpec((rows, width), seq)] * 2
            + [pl.BlockSpec((rows, d), seq)],
        ),
        out_shape=[wide, wide, wide, tall, tall, jax.ShapeDtypeStruct((row_len, d), BF16)],
        input_output_aliases=aliases,
        compiler_params=pltpu.CompilerParams(vmem_limit_bytes=60 * MIB),
        cost_estimate=cost(9),
        name="project",
    )(*args)


def gelu_parts(v):
    t = 1.0 / (1.0 + (0.3275911 * 0.7071067811865476) * jnp.abs(v))
    bell = jnp.exp(-0.5 * (v * v))
    poly = t * (0.127414796 + t * (-0.142248368 + t * (0.7107068705 + t * (-0.7265760135 + t * 0.5307027145))))
    tail = poly * bell
    below = jnp.where(v < 0.0, tail, 1.0 - tail)
    return v * below, below + v * (bell * 0.3989422804014327)


def mlp_body(*refs, first, again, rows, skip):
    tok_ref, g_ref, gain_ref, shift_ref, w1_ref, b1_ref, w2_ref = refs[:7]
    refs = refs[7:]
    if not first:
        dw1_in, dw2_in = refs[:2]
        refs = refs[2:]
    if again:
        out_in, e_in = refs[:2]
        refs = refs[2:]
    refs = refs[skip:]
    out_ref, e_ref, dw1_ref, dw2_ref, db1_ref, dgain_ref, dshift_ref = refs[:7]
    normed, normed_t, out_acc, back_acc, act_t, pre_t = refs[7:]
    step = pl.program_id(0)
    last = pl.num_programs(0) - 1
    half, d = normed.shape
    blocks = half // rows

    @pl.when(step == 0)
    def _():
        def prepare(i, _):
            at = pl.ds(pl.multiple_of(i * rows, rows), rows)
            centred, rstd = norm_stats(tok_ref[at, :].astype(F32))
            n = (centred * rstd * gain_ref[...] + shift_ref[...]).astype(BF16)
            normed[at, :] = n
            normed_t[:, at] = n.T
            return 0

        lax.fori_loop(0, blocks, prepare, 0)
        dgain_ref[...] = jnp.zeros_like(dgain_ref)
        dshift_ref[...] = jnp.zeros_like(dshift_ref)

    def forward(i, bias_sum):
        at = pl.ds(pl.multiple_of(i * rows, rows), rows)
        v = dot(normed[at, :], w1_ref[...]) + b1_ref[...]
        grad_act = dot(g_ref[at, :], w2_ref[...], NT)
        act, slope = gelu_parts(v)
        act = act.astype(BF16)
        grad_pre = (grad_act * slope).astype(BF16)
        out = dot(act, w2_ref[...])
        back = dot(grad_pre, w1_ref[...], NT)

        @pl.when(step == 0)
        def _():
            out_acc[at, :] = out
            back_acc[at, :] = back

        @pl.when(step > 0)
        def _():
            out_acc[at, :] += out
            back_acc[at, :] += back

        act_t[:, at] = act.T
        pre_t[at, :] = grad_pre
        return bias_sum + jnp.sum(grad_pre.astype(F32), axis=0, keepdims=True)

    db1_ref[...] = lax.fori_loop(0, blocks, forward, jnp.zeros(db1_ref.shape, F32))

    def weights(i, _):
        at = pl.ds(pl.multiple_of(i * rows, rows), rows)
        one = dot(normed_t[at, :], pre_t[...])
        if not first:
            one = one + dw1_in[at, :].astype(F32)
        dw1_ref[at, :] = one.astype(BF16)
        two = dot(act_t[...], g_ref[:, at])
        if not first:
            two = two + dw2_in[:, at].astype(F32)
        dw2_ref[:, at] = two.astype(BF16)
        return 0

    for i in range(d // rows):
        weights(i, 0)

    @pl.when(step == last)
    def _():
        def finish(i, _):
            at = pl.ds(pl.multiple_of(i * rows, rows), rows)
            centred, rstd = norm_stats(tok_ref[at, :].astype(F32))
            back = back_acc[at, :]
            dgain_ref[...] += jnp.sum(back * (centred * rstd), axis=0, keepdims=True)
            dshift_ref[...] += jnp.sum(back, axis=0, keepdims=True)
            e, out = back * gain_ref[...], out_acc[at, :]
            if again:
                e, out = e + e_in[at, :].astype(F32), out + out_in[at, :].astype(F32)
            e_ref[at, :] = e.astype(BF16)
            out_ref[at, :] = out.astype(BF16)
            return 0

        lax.fori_loop(0, blocks, finish, 0)


def mlp(tok, g, gain, shift, w1, b1, w2, chunk, rows, span, before=None, partial=None, after=()):
    half, d = tok.shape
    base, chunks = span
    hidden = chunks * chunk
    fixed = lambda j: (0, 0)
    cols = pl.BlockSpec((d, chunk), lambda j: (0, j))
    tall = pl.BlockSpec((chunk, d), lambda j: (j, 0))
    whole = pl.BlockSpec((half, d), fixed)
    line = pl.BlockSpec((1, d), fixed)
    bias = pl.BlockSpec((1, chunk), lambda j: (0, j))
    cols_in = pl.BlockSpec((d, chunk), lambda j: (0, base + j))
    tall_in = pl.BlockSpec((chunk, d), lambda j: (base + j, 0))
    args = [tok, g, gain, shift, w1, b1, w2]
    specs = [whole, whole, line, line, cols_in, pl.BlockSpec((1, chunk), lambda j: (0, base + j)), tall_in]
    if before is not None:
        args += list(before)
        specs += [cols_in, tall_in]
    if partial is not None:
        args += list(partial)
        specs += [whole, whole]
    args += list(after)
    specs += [pl.BlockSpec(memory_space=pl.ANY)] * len(after)
    shape = jax.ShapeDtypeStruct
    return pl.pallas_call(
        functools.partial(mlp_body, first=before is None, again=partial is not None, rows=rows, skip=len(after)),
        grid=(chunks,),
        in_specs=specs,
        out_specs=[whole, whole, cols, tall, bias, line, line],
        out_shape=[
            shape((half, d), BF16),
            shape((half, d), BF16),
            shape((d, hidden), BF16),
            shape((hidden, d), BF16),
            shape((1, hidden), F32),
            shape((1, d), F32),
            shape((1, d), F32),
        ],
        scratch_shapes=[
            pltpu.VMEM((half, d), BF16),
            pltpu.VMEM((d, half), BF16),
            pltpu.VMEM((half, d), F32),
            pltpu.VMEM((half, d), F32),
            pltpu.VMEM((chunk, half), BF16),
            pltpu.VMEM((half, chunk), BF16),
        ],
        compiler_params=pltpu.CompilerParams(vmem_limit_bytes=60 * MIB),
        cost_estimate=cost(44 * hidden / w1.shape[1]),
        name="feed_forward",
    )(*args)


def fold(x, op):
    return op(x.reshape(x.shape[0] // 8, 8, x.shape[1]), axis=0)


def attention_body(info_ref, q_ref, kt, vt, do_ref, k_ref, v_ref, start_ref, cosq_ref, sinq_ref, *rest, first, block, skip):
    if first:
        rest = rest[skip:]
        o_ref, dq_ref, dk_ref, dv_ref, s_scr, e_scr = rest
    else:
        cos_ref, sin_ref, dq_in, dk_in, dv_in = rest[:5]
        o_ref, grads_ref, s_scr, e_scr, dk_ref, dv_ref = rest[5 + skip :]
    step = pl.program_id(1)
    half = pl.num_programs(1) * block
    place = info_ref[0] * pl.num_programs(1) + step
    row_len = kt.shape[1]

    @pl.when(step == 0)
    def _():
        if first:
            dk_ref[...] = jnp.zeros_like(dk_ref)
            dv_ref[...] = jnp.zeros_like(dv_ref)
        else:
            dk_ref[...] = dk_in[...]
            dv_ref[...] = dv_in[...]

    q_t = q_ref[...]
    zeros = jnp.zeros((HEAD, block), BF16)
    q_wide = [jnp.concatenate([q_t[:HEAD], zeros], 0), jnp.concatenate([zeros, q_t[HEAD:]], 0)]
    start = start_ref[...]
    spot = place * block + lax.broadcasted_iota(jnp.int32, (1, block), 1)
    low = info_ref[1 + step]
    high = place + 1
    rows = lax.broadcasted_iota(jnp.int32, (block, block // 2), 0)

    def scores(kb, tops):
        tops = list(tops)
        off = pl.multiple_of(kb * block, block)
        k_blk = k_ref[pl.ds(off, block), :]
        for w in range(2):
            at = slice(w * block // 2, (w + 1) * block // 2)
            legal = (rows >= start[:, at] - off) & (rows <= spot[:, at] - off)
            for h in range(2):
                s = jnp.where(legal, dot(k_blk, q_wide[h][:, at]), MASKED_SCORE)
                s_scr[h, pl.ds(off, block), at] = s
                tops[2 * h + w] = jnp.maximum(tops[2 * h + w], fold(s, jnp.max))
        return tuple(tops)

    tops = lax.fori_loop(low, high, scores, (jnp.full((8, block // 2), MASKED_SCORE, F32),) * 4)
    top = [jnp.max(jnp.concatenate(tops[2 * h : 2 * h + 2], 1), axis=0, keepdims=True) for h in range(2)]

    def forward(kb, carry):
        carry = list(carry)
        off = pl.multiple_of(kb * block, block)
        for h in range(2):
            e = jnp.exp(s_scr[h, pl.ds(off, block), :] - top[h])
            carry[h] = carry[h] + fold(e, jnp.sum)
            e = e.astype(BF16)
            e_scr[h, pl.ds(off, block), :] = e
            carry[2 + h] = carry[2 + h] + dot(vt[h * HEAD : (h + 1) * HEAD, pl.ds(off, block)], e)
        return tuple(carry)

    eight, tall = jnp.zeros((8, block), F32), jnp.zeros((HEAD, block), F32)
    sums = lax.fori_loop(low, high, forward, (eight, eight, tall, tall))
    grad = do_ref[...].astype(F32)
    centre, grad_low, grad_wide = [], [], []
    for h in range(2):
        at = slice(h * HEAD, (h + 1) * HEAD)
        inverse = 1.0 / jnp.sum(sums[h], axis=0, keepdims=True)
        o = sums[2 + h] * inverse
        o_ref[at, :] = o.astype(BF16)
        scaled = grad[at] * inverse
        centre.append(jnp.sum(scaled * o, axis=0, keepdims=True))
        grad_low.append(scaled.astype(BF16))
    grad_wide = [jnp.concatenate([grad_low[0], zeros], 0), jnp.concatenate([zeros, grad_low[1]], 0)]

    def backward(kb, carry):
        carry = list(carry)
        off = pl.multiple_of(kb * block, block)
        here = pl.ds(off, block)
        v_blk = v_ref[here, :]
        for h in range(2):
            at = slice(h * HEAD, (h + 1) * HEAD)
            e = e_scr[h, here, :]
            ds = (e.astype(F32) * (dot(v_blk, grad_wide[h]) - centre[h])).astype(BF16)
            dv_ref[at, here] += dot(grad_low[h], e, NT)
            dk_ref[at, here] += dot(q_t[at], ds, NT)
            carry[h] = carry[h] + dot(kt[at, here], ds)
        return tuple(carry)

    grads = lax.fori_loop(low, high, backward, (tall, tall))
    turned = [turn(grads[h] * SCALING, cosq_ref[...], -sinq_ref[...]).astype(BF16) for h in range(2)]
    if first:
        dq_ref[...] = jnp.concatenate(turned, 0)
    else:
        off = pl.multiple_of(place * block, block)
        grads_ref[0, :, pl.ds(off, block)] = jnp.concatenate(turned, 0)

        @pl.when(step == pl.num_programs(1) - 1)
        def _():
            other = pl.multiple_of((1 - info_ref[0]) * half, half)
            grads_ref[0, :, pl.ds(other, half)] = dq_in[...]

            def finish(i, _):
                here = pl.ds(pl.multiple_of(i * block, block), block)
                cosine, sine = cos_ref[:, here], -sin_ref[:, here]
                for h in range(2):
                    at = slice(h * HEAD, (h + 1) * HEAD)
                    grads_ref[1, at, here] = turn(dk_ref[at, here], cosine, sine).astype(BF16)
                grads_ref[2, :, here] = dv_ref[:, here].astype(BF16)
                return 0

            lax.fori_loop(0, row_len // block, finish, 0)


def attention(info, group, q_t, k_t, v_t, do_t, k, v, start, cosine, sine, before, base_in=0, after=()):
    base, pairs = group
    width = pairs * PAIR
    row_len = q_t.shape[1]
    half = do_t.shape[1]
    block = 512
    steps = half // block
    first = before is None
    place = lambda p, i, info: (base + p, info[0] * steps + i)
    line = lambda p, i, info: (0, info[0] * steps + i)
    here = pl.BlockSpec((PAIR, block), lambda p, i, info: (p, i))
    wide = pl.BlockSpec((PAIR, row_len), lambda p, i, info: (p, 0))
    of_row = pl.BlockSpec((PAIR, row_len), lambda p, i, info: (base + p, 0))
    here_in = pl.BlockSpec((PAIR, block), lambda p, i, info: (base + p, i))
    tall = pl.BlockSpec((row_len, PAIR), lambda p, i, info: (0, base + p))
    angle = pl.BlockSpec((ROT // 2, block), line)
    args = [info, q_t, k_t, v_t, do_t, k, v, start, cosine, sine]
    specs = [pl.BlockSpec((PAIR, block), place), of_row, of_row, here_in, tall, tall, pl.BlockSpec((1, block), line), angle, angle]
    shape = jax.ShapeDtypeStruct
    scratch = [pltpu.VMEM((2, row_len, block), F32), pltpu.VMEM((2, row_len, block), BF16)]
    if first:
        outs = [shape((width, half), BF16)] * 2 + [shape((width, row_len), F32)] * 2
        out_specs = [here, here, wide, wide]
    else:
        table = pl.BlockSpec((ROT // 2, row_len), lambda p, i, info: (0, 0))
        args += [cosine, sine, *before]
        wide_in = pl.BlockSpec((PAIR, row_len), lambda p, i, info: (base_in + p, 0))
        specs += [table, table, pl.BlockSpec((PAIR, half), lambda p, i, info: (base_in + p, 0)), wide_in, wide_in]
        outs = [shape((width, half), BF16), shape((3, width, row_len), BF16)]
        out_specs = [here, pl.BlockSpec((3, PAIR, row_len), lambda p, i, info: (0, p, 0))]
        scratch += [pltpu.VMEM((PAIR, row_len), F32)] * 2
    args += list(after)
    specs += [pl.BlockSpec(memory_space=pl.ANY)] * len(after)
    return pl.pallas_call(
        functools.partial(attention_body, first=first, block=block, skip=len(after)),
        grid_spec=pltpu.PrefetchScalarGridSpec(
            num_scalar_prefetch=1,
            grid=(pairs, steps),
            in_specs=specs,
            out_specs=out_specs,
            scratch_shapes=scratch,
        ),
        out_shape=outs,
        compiler_params=pltpu.CompilerParams(vmem_limit_bytes=60 * MIB),
        cost_estimate=cost(11 * pairs),
        name="attention",
    )(*args)


def exchange(x, bit):
    return lax.ppermute(x, "dp", [(i, i ^ (1 << bit)) for i in range(lax.axis_size("dp"))])


def orders():
    bits = range(lax.axis_size("dp").bit_length() - 1)
    return [0, *bits[1:]], [0, *bits[2:], 1]


class Sum:
    def __init__(self, x, order):
        self.x = x
        self.stages = [(True, bit) for bit in order] + [(False, bit) for bit in order[::-1]]
        self.sent = None

    def start(self):
        if not self.stages:
            return
        halving, bit = self.stages[0]
        mine = (lax.axis_index("dp") >> bit) & 1
        if halving:
            half = self.x.shape[0] // 2
            self.sent = exchange(lax.dynamic_slice_in_dim(self.x, (1 - mine) * half, half, 0), bit)
        else:
            self.sent = exchange(self.x, bit)

    def finish(self):
        if self.sent is None:
            return
        halving, bit = self.stages.pop(0)
        mine = (lax.axis_index("dp") >> bit) & 1
        if halving:
            half = self.x.shape[0] // 2
            kept = lax.dynamic_slice_in_dim(self.x, mine * half, half, 0)
            self.x = (kept.astype(F32) + self.sent.astype(F32)).astype(BF16)
        else:
            low = jnp.concatenate([self.x, self.sent], 0)
            high = jnp.concatenate([self.sent, self.x], 0)
            self.x = jnp.where(mine == 0, low, high)
        self.sent = None


def tick(*sums):
    for s in sums:
        s.finish()
    arrived = tuple(s.x for s in sums)
    for s in sums:
        s.start()
    return arrived


def small_total(x):
    for bit in orders()[0]:
        x = x + exchange(x, bit)
    return x


def per_device(
    tokens,
    cotangent,
    lengths,
    pad_count,
    ln1_gain,
    ln1_bias,
    ln2_gain,
    ln2_bias,
    qkv_weight,
    qkv_bias,
    out_weight,
    out_bias,
    fc1_weight,
    fc1_bias,
    fc2_weight,
):
    half, d = tokens.shape
    row_len = half * lax.axis_size("mp")
    width = qkv_weight.shape[2]
    hidden = fc1_weight.shape[1]
    me = lax.axis_index("mp")
    swap = [(0, 1), (1, 0)]
    y_first, z_first = orders()
    tok_far = lax.ppermute(tokens, "mp", swap)

    docs = lengths.shape[1]
    order = jnp.arange(docs)
    starts = jnp.sum(jnp.where(order[None, :] < order[:, None], lengths[0][None, :], 0), axis=1)
    places = jnp.arange(row_len, dtype=jnp.int32)
    doc_start = jnp.max(jnp.where(starts[:, None] <= places[None, :], starts[:, None], 0), axis=0)
    kept = row_len - pad_count[0]
    start = jnp.where(places < kept, doc_start, places).astype(jnp.int32)
    frequency = ROTARY_BASE ** (-(jnp.arange(ROT // 2, dtype=F32) * 2.0) / ROT)
    angles = frequency[:, None] * (places - doc_start).astype(F32)[None, :]
    cosine, sine = jnp.cos(angles), jnp.sin(angles)
    block = 512
    lows = (start[::block] // block).astype(jnp.int32).reshape(2, -1)
    near = jnp.concatenate([me[None].astype(jnp.int32), lows[me]])
    far = jnp.concatenate([(1 - me)[None].astype(jnp.int32), lows[1 - me]])
    cot_later, tok_far = lax.optimization_barrier((cotangent, tok_far))
    cot_far = lax.ppermute(cot_later, "mp", swap)
    inside = jnp.arange(half, dtype=jnp.int32)[:, None]
    g_near = jnp.where(inside < kept - me * half, cotangent, jnp.zeros((), BF16))
    g_far = jnp.where(inside < kept - (1 - me) * half, cot_far, jnp.zeros((), BF16))

    gain1, shift1 = ln1_gain[None], ln1_bias[None]
    gain2, shift2 = ln2_gain[None], ln2_bias[None]
    w_t = jnp.transpose(qkv_weight, (1, 2, 0)).reshape(3 * width, d)
    b_col = qkv_bias.reshape(3 * width, 1)
    b1 = fc1_bias[None]

    feed = (gain2, shift2, fc1_weight, b1, fc2_weight)
    wide = hidden // 2
    mlp_near = mlp(tokens, g_near, *feed, wide, 256, (0, 2))
    front = (gain1, shift1, w_t, b_col, cosine, sine, row_len)
    made = project(near[:1], tokens, *front, None)
    q_t, k_t, v_t, k, v, normed1 = project(far[:1], tok_far, *front, made)
    do_near = dot(out_weight, g_near, NT).astype(BF16)
    do_far = dot(out_weight, g_far, NT).astype(BF16)

    def attend(which, group, before, base_in, do_t, after=()):
        return attention(which, group, q_t, k_t, v_t, do_t, k, v, start[None], cosine, sine, before, base_in, after)

    def branch(o, part):
        return dot(o, out_weight, TN) + part.astype(F32)

    every = (0, width // PAIR)
    o_near, *kept_near = attend(near, every, None, 0, do_near)
    mlp_far = mlp(tok_far, g_far, *feed, wide, 256, (0, 2), mlp_near[2:4], None, (o_near,))
    out_far, e2_far = mlp_far[:2]
    grad_fc1, grad_fc2 = lax.psum(mlp_far[2:4], "dp")

    def rest(g_near, g_far, tok_near, tok_far, normed1, w_t, o_near, kept_near, out_near, out_far, e2_near, e2_far, do_far, early, fc1_b):
        o_far, grads = attend(far, every, kept_near, 0, do_far)
        grads = grads.reshape(3 * width, row_len)
        qkv = dot(grads, normed1).astype(BF16)
        out = (dot(o_near, g_near) + dot(o_far, g_far)).astype(BF16)
        arrived = lax.ppermute(branch(o_far, out_far).astype(BF16), "mp", swap)

        def norm_back(place, tok, e2):
            part = lax.dynamic_slice_in_dim(grads, place * half, half, 1)
            back = dot(part, w_t, TN)
            centred, rstd = norm_stats(tok.astype(F32))
            xhat = centred * rstd
            return gain1 * back + e2.astype(F32), jnp.sum(back * xhat, axis=0), jnp.sum(back, axis=0)

        e_far, dgain_far, dshift_far = norm_back(1 - me, tok_far, e2_far)
        e_arrived = lax.ppermute(e_far.astype(BF16), "mp", swap)
        e_near, dgain_near, dshift_near = norm_back(me, tok_near, e2_near)
        late = jnp.stack([dgain_near + dgain_far, dshift_near + dshift_far])
        small = jnp.concatenate([late.reshape(-1), early.reshape(-1), jnp.sum(grads.astype(F32), axis=1), fc1_b])
        small = small_total(small.reshape(-1, 128)).reshape(-1)
        both = small[: 5 * d].reshape(5, d)

        cut = width
        parts = [(out, y_first), (qkv[:cut], z_first), (qkv[cut : 2 * cut], y_first), (qkv[2 * cut :], y_first)]
        parts = [Sum(x, order) for x, order in parts]
        while any(p.stages for p in parts):
            tick(*parts)

        inputs = tok_near.astype(F32)
        output = (inputs + (branch(o_near, out_near) + arrived.astype(F32)) + out_bias).astype(BF16)
        e = e_near + e_arrived.astype(F32)
        centred, rstd = norm_stats(inputs)
        xhat = centred * rstd
        grad_in = rstd * (e - jnp.mean(e, axis=-1, keepdims=True) - xhat * jnp.mean(e * xhat, axis=-1, keepdims=True))
        grad_tokens = g_near.astype(F32) + grad_in
        both = both + lax.ppermute(both, "mp", swap)
        grad_qkv = jnp.transpose(jnp.stack([p.x for p in parts[1:]]), (2, 0, 1)).astype(F32)
        grad_out_w = parts[0].x.astype(F32)
        return output, grad_tokens, both, small[5 * d :], grad_qkv, grad_out_w

    def never(g_near, g_far, tok_near, *unused):
        zeros = jnp.zeros
        return (
            tok_near,
            zeros((half, d), F32),
            zeros((5, d), F32),
            zeros((3 * width + hidden,), F32),
            zeros((d, 3, width), F32),
            zeros((width, d), F32),
        )

    early = jnp.stack([(mlp_near[5] + mlp_far[5])[0], (mlp_near[6] + mlp_far[6])[0], jnp.sum(g_near.astype(F32), axis=0)])
    fc1_b = (mlp_near[4] + mlp_far[4])[0]
    output, grad_tokens, both, small, grad_qkv, grad_out_w = lax.cond(
        jnp.min(lengths) > 0,
        rest,
        never,
        g_near,
        g_far,
        tokens,
        tok_far,
        normed1,
        w_t,
        o_near,
        kept_near,
        mlp_near[0],
        out_far,
        mlp_near[1],
        e2_far,
        do_far,
        early,
        fc1_b,
    )
    grad_qkv_b = small[: 3 * width].reshape(3, width)
    grad_fc1_b = small[3 * width :]
    return (
        output,
        grad_tokens,
        both[0],
        both[1],
        both[2],
        both[3],
        grad_qkv,
        grad_qkv_b,
        grad_out_w,
        both[4],
        grad_fc1.astype(F32),
        grad_fc1_b,
        grad_fc2.astype(F32),
    )


def solution(mesh):
    return jax.shard_map(
        per_device,
        mesh=mesh,
        in_specs=(
            P(("dp", "mp"), None),
            P(("dp", "mp"), None),
            P("dp", None),
            P("dp"),
            P(),
            P(),
            P(),
            P(),
            P(None, None, "mp"),
            P(None, "mp"),
            P("mp", None),
            P(),
            P(None, "mp"),
            P("mp"),
            P("mp", None),
        ),
        out_specs=(
            P(("dp", "mp"), None),
            P(("dp", "mp"), None),
            P(),
            P(),
            P(),
            P(),
            P(None, None, "mp"),
            P(None, "mp"),
            P("mp", None),
            P(),
            P(None, "mp"),
            P("mp"),
            P("mp", None),
        ),
        check_vma=False,
    )
```

```python
import functools

import jax
import jax.numpy as jnp
from jax import lax
from jax.experimental import pallas as pl
from jax.experimental.pallas import tpu as pltpu
from jax.sharding import PartitionSpec as P

HEAD = 64
ROT = 16
PAIR = 2 * HEAD
EPSILON = 1e-05
MASKED_SCORE = -1e30
ROTARY_BASE = 10000.0
SCALING = HEAD**-0.5
F32 = jnp.float32
BF16 = jnp.bfloat16
NN = ((1,), (0,))
NT = ((1,), (1,))
TN = ((0,), (0,))
MIB = 2**20


def dot(a, b, dims=NN):
    return lax.dot_general(a, b, (dims, ((), ())), preferred_element_type=F32)


def cost(micros):
    return pl.CostEstimate(flops=int(micros * 1.1e9), bytes_accessed=0, transcendentals=0)


def norm_stats(v):
    average = jnp.mean(v, axis=-1, keepdims=True)
    centred = v - average
    spread = jnp.mean(centred * centred, axis=-1, keepdims=True)
    return centred, lax.rsqrt(spread + EPSILON)


def turn(x, cosine, sine):
    half = ROT // 2
    u, w = x[:half], x[half:ROT]
    return jnp.concatenate([u * cosine - w * sine, w * cosine + u * sine, x[ROT:]], axis=0)


def project_body(place_ref, tok_ref, gain_ref, shift_ref, w_ref, b_ref, cos_ref, sin_ref, *rest):
    q_out, kt_out, vt_out, k_out, v_out, n_out = rest[-6:]
    x = tok_ref[...].astype(F32)
    centred, rstd = norm_stats(x)
    normed = (centred * rstd * gain_ref[...] + shift_ref[...]).astype(BF16)
    n_out[...] = normed
    cosine, sine = cos_ref[...], sin_ref[...]
    width = k_out.shape[1]

    def head_rows(c, scale):
        p = dot(w_ref[c * width : (c + 1) * width, :], normed, NT) + b_ref[c * width : (c + 1) * width, :]
        if c == 2:
            return p.astype(BF16)
        parts = [turn(p[h : h + HEAD], cosine, sine) for h in range(0, width, HEAD)]
        return (jnp.concatenate(parts, axis=0) * scale).astype(BF16)

    q_out[...] = head_rows(0, SCALING)
    k = head_rows(1, 1.0)
    kt_out[...] = k
    k_out[...] = k.T
    v = head_rows(2, 1.0)
    vt_out[...] = v
    v_out[...] = v.T


def project(place, tok, gain, shift, w_t, b_col, cosine, sine, row_len, before, after=()):
    half, d = tok.shape
    width = w_t.shape[0] // 3
    rows = 256
    steps = half // rows
    here = lambda i, place: (i, 0)
    lanes = lambda i, place: (0, place[0] * steps + i)
    seq = lambda i, place: (place[0] * steps + i, 0)
    fixed = lambda i, place: (0, 0)
    specs = [
        pl.BlockSpec((rows, d), here),
        pl.BlockSpec((1, d), fixed),
        pl.BlockSpec((1, d), fixed),
        pl.BlockSpec((3 * width, d), fixed),
        pl.BlockSpec((3 * width, 1), fixed),
        pl.BlockSpec((ROT // 2, rows), lanes),
        pl.BlockSpec((ROT // 2, rows), lanes),
    ]
    args = [place, tok, gain, shift, w_t, b_col, cosine, sine]
    aliases = {}
    if before is not None:
        specs += [pl.BlockSpec(memory_space=pl.ANY)] * 6
        aliases = {len(args) + i: i for i in range(6)}
        args += list(before)
    args += list(after)
    specs += [pl.BlockSpec(memory_space=pl.ANY)] * len(after)
    wide = jax.ShapeDtypeStruct((width, row_len), BF16)
    tall = jax.ShapeDtypeStruct((row_len, width), BF16)
    return pl.pallas_call(
        project_body,
        grid_spec=pltpu.PrefetchScalarGridSpec(
            num_scalar_prefetch=1,
            grid=(steps,),
            in_specs=specs,
            out_specs=[pl.BlockSpec((width, rows), lanes)] * 3
            + [pl.BlockSpec((rows, width), seq)] * 2
            + [pl.BlockSpec((rows, d), seq)],
        ),
        out_shape=[wide, wide, wide, tall, tall, jax.ShapeDtypeStruct((row_len, d), BF16)],
        input_output_aliases=aliases,
        compiler_params=pltpu.CompilerParams(vmem_limit_bytes=60 * MIB),
        cost_estimate=cost(9),
        name="project",
    )(*args)


def gelu_parts(v):
    t = 1.0 / (1.0 + (0.3275911 * 0.7071067811865476) * jnp.abs(v))
    bell = jnp.exp(-0.5 * (v * v))
    poly = t * (0.127414796 + t * (-0.142248368 + t * (0.7107068705 + t * (-0.7265760135 + t * 0.5307027145))))
    tail = poly * bell
    below = jnp.where(v < 0.0, tail, 1.0 - tail)
    return v * below, below + v * (bell * 0.3989422804014327)


def mlp_body(*refs, first, again, rows, skip):
    tok_ref, g_ref, gain_ref, shift_ref, w1_ref, b1_ref, w2_ref = refs[:7]
    refs = refs[7:]
    if not first:
        dw1_in, dw2_in = refs[:2]
        refs = refs[2:]
    if again:
        out_in, e_in = refs[:2]
        refs = refs[2:]
    refs = refs[skip:]
    out_ref, e_ref, dw1_ref, dw2_ref, db1_ref, dgain_ref, dshift_ref = refs[:7]
    normed, normed_t, out_acc, back_acc, act_t, pre_t = refs[7:]
    step = pl.program_id(0)
    last = pl.num_programs(0) - 1
    half, d = normed.shape
    blocks = half // rows

    @pl.when(step == 0)
    def _():
        def prepare(i, _):
            at = pl.ds(pl.multiple_of(i * rows, rows), rows)
            centred, rstd = norm_stats(tok_ref[at, :].astype(F32))
            n = (centred * rstd * gain_ref[...] + shift_ref[...]).astype(BF16)
            normed[at, :] = n
            normed_t[:, at] = n.T
            return 0

        lax.fori_loop(0, blocks, prepare, 0)
        dgain_ref[...] = jnp.zeros_like(dgain_ref)
        dshift_ref[...] = jnp.zeros_like(dshift_ref)

    def forward(i, bias_sum):
        at = pl.ds(pl.multiple_of(i * rows, rows), rows)
        v = dot(normed[at, :], w1_ref[...]) + b1_ref[...]
        grad_act = dot(g_ref[at, :], w2_ref[...], NT)
        act, slope = gelu_parts(v)
        act = act.astype(BF16)
        grad_pre = (grad_act * slope).astype(BF16)
        out = dot(act, w2_ref[...])
        back = dot(grad_pre, w1_ref[...], NT)

        @pl.when(step == 0)
        def _():
            out_acc[at, :] = out
            back_acc[at, :] = back

        @pl.when(step > 0)
        def _():
            out_acc[at, :] += out
            back_acc[at, :] += back

        act_t[:, at] = act.T
        pre_t[at, :] = grad_pre
        return bias_sum + jnp.sum(grad_pre.astype(F32), axis=0, keepdims=True)

    db1_ref[...] = lax.fori_loop(0, blocks, forward, jnp.zeros(db1_ref.shape, F32))

    def weights(i, _):
        at = pl.ds(pl.multiple_of(i * rows, rows), rows)
        one = dot(normed_t[at, :], pre_t[...])
        if not first:
            one = one + dw1_in[at, :].astype(F32)
        dw1_ref[at, :] = one.astype(BF16)
        two = dot(act_t[...], g_ref[:, at])
        if not first:
            two = two + dw2_in[:, at].astype(F32)
        dw2_ref[:, at] = two.astype(BF16)
        return 0

    for i in range(d // rows):
        weights(i, 0)

    @pl.when(step == last)
    def _():
        def finish(i, _):
            at = pl.ds(pl.multiple_of(i * rows, rows), rows)
            centred, rstd = norm_stats(tok_ref[at, :].astype(F32))
            back = back_acc[at, :]
            dgain_ref[...] += jnp.sum(back * (centred * rstd), axis=0, keepdims=True)
            dshift_ref[...] += jnp.sum(back, axis=0, keepdims=True)
            e, out = back * gain_ref[...], out_acc[at, :]
            if again:
                e, out = e + e_in[at, :].astype(F32), out + out_in[at, :].astype(F32)
            e_ref[at, :] = e.astype(BF16)
            out_ref[at, :] = out.astype(BF16)
            return 0

        lax.fori_loop(0, blocks, finish, 0)


def mlp(tok, g, gain, shift, w1, b1, w2, chunk, rows, span, before=None, partial=None, after=()):
    half, d = tok.shape
    base, chunks = span
    hidden = chunks * chunk
    fixed = lambda j: (0, 0)
    cols = pl.BlockSpec((d, chunk), lambda j: (0, j))
    tall = pl.BlockSpec((chunk, d), lambda j: (j, 0))
    whole = pl.BlockSpec((half, d), fixed)
    line = pl.BlockSpec((1, d), fixed)
    bias = pl.BlockSpec((1, chunk), lambda j: (0, j))
    cols_in = pl.BlockSpec((d, chunk), lambda j: (0, base + j))
    tall_in = pl.BlockSpec((chunk, d), lambda j: (base + j, 0))
    args = [tok, g, gain, shift, w1, b1, w2]
    specs = [whole, whole, line, line, cols_in, pl.BlockSpec((1, chunk), lambda j: (0, base + j)), tall_in]
    if before is not None:
        args += list(before)
        specs += [cols_in, tall_in]
    if partial is not None:
        args += list(partial)
        specs += [whole, whole]
    args += list(after)
    specs += [pl.BlockSpec(memory_space=pl.ANY)] * len(after)
    shape = jax.ShapeDtypeStruct
    return pl.pallas_call(
        functools.partial(mlp_body, first=before is None, again=partial is not None, rows=rows, skip=len(after)),
        grid=(chunks,),
        in_specs=specs,
        out_specs=[whole, whole, cols, tall, bias, line, line],
        out_shape=[
            shape((half, d), BF16),
            shape((half, d), BF16),
            shape((d, hidden), BF16),
            shape((hidden, d), BF16),
            shape((1, hidden), F32),
            shape((1, d), F32),
            shape((1, d), F32),
        ],
        scratch_shapes=[
            pltpu.VMEM((half, d), BF16),
            pltpu.VMEM((d, half), BF16),
            pltpu.VMEM((half, d), F32),
            pltpu.VMEM((half, d), F32),
            pltpu.VMEM((chunk, half), BF16),
            pltpu.VMEM((half, chunk), BF16),
        ],
        compiler_params=pltpu.CompilerParams(vmem_limit_bytes=60 * MIB),
        cost_estimate=cost(44 * hidden / w1.shape[1]),
        name="feed_forward",
    )(*args)


def fold(x, op):
    return op(x.reshape(x.shape[0] // 8, 8, x.shape[1]), axis=0)


def attention_body(info_ref, q_ref, kt, vt, do_ref, k_ref, v_ref, start_ref, cosq_ref, sinq_ref, *rest, first, block, skip):
    if first:
        rest = rest[skip:]
        o_ref, dq_ref, dk_ref, dv_ref, s_scr, e_scr = rest
    else:
        cos_ref, sin_ref, dq_in, dk_in, dv_in = rest[:5]
        o_ref, grads_ref, s_scr, e_scr, dk_ref, dv_ref = rest[5 + skip :]
    step = pl.program_id(1)
    half = pl.num_programs(1) * block
    place = info_ref[0] * pl.num_programs(1) + step
    row_len = kt.shape[1]

    @pl.when(step == 0)
    def _():
        if first:
            dk_ref[...] = jnp.zeros_like(dk_ref)
            dv_ref[...] = jnp.zeros_like(dv_ref)
        else:
            dk_ref[...] = dk_in[...]
            dv_ref[...] = dv_in[...]

    q_t = q_ref[...]
    zeros = jnp.zeros((HEAD, block), BF16)
    q_wide = [jnp.concatenate([q_t[:HEAD], zeros], 0), jnp.concatenate([zeros, q_t[HEAD:]], 0)]
    start = start_ref[...]
    spot = place * block + lax.broadcasted_iota(jnp.int32, (1, block), 1)
    low = info_ref[1 + step]
    high = place + 1
    rows = lax.broadcasted_iota(jnp.int32, (block, block // 2), 0)

    def scores(kb, tops):
        tops = list(tops)
        off = pl.multiple_of(kb * block, block)
        k_blk = k_ref[pl.ds(off, block), :]
        for w in range(2):
            at = slice(w * block // 2, (w + 1) * block // 2)
            legal = (rows >= start[:, at] - off) & (rows <= spot[:, at] - off)
            for h in range(2):
                s = jnp.where(legal, dot(k_blk, q_wide[h][:, at]), MASKED_SCORE)
                s_scr[h, pl.ds(off, block), at] = s
                tops[2 * h + w] = jnp.maximum(tops[2 * h + w], fold(s, jnp.max))
        return tuple(tops)

    tops = lax.fori_loop(low, high, scores, (jnp.full((8, block // 2), MASKED_SCORE, F32),) * 4)
    top = [jnp.max(jnp.concatenate(tops[2 * h : 2 * h + 2], 1), axis=0, keepdims=True) for h in range(2)]

    def forward(kb, carry):
        carry = list(carry)
        off = pl.multiple_of(kb * block, block)
        for h in range(2):
            e = jnp.exp(s_scr[h, pl.ds(off, block), :] - top[h])
            carry[h] = carry[h] + fold(e, jnp.sum)
            e = e.astype(BF16)
            e_scr[h, pl.ds(off, block), :] = e
            carry[2 + h] = carry[2 + h] + dot(vt[h * HEAD : (h + 1) * HEAD, pl.ds(off, block)], e)
        return tuple(carry)

    eight, tall = jnp.zeros((8, block), F32), jnp.zeros((HEAD, block), F32)
    sums = lax.fori_loop(low, high, forward, (eight, eight, tall, tall))
    grad = do_ref[...].astype(F32)
    centre, grad_low, grad_wide = [], [], []
    for h in range(2):
        at = slice(h * HEAD, (h + 1) * HEAD)
        inverse = 1.0 / jnp.sum(sums[h], axis=0, keepdims=True)
        o = sums[2 + h] * inverse
        o_ref[at, :] = o.astype(BF16)
        scaled = grad[at] * inverse
        centre.append(jnp.sum(scaled * o, axis=0, keepdims=True))
        grad_low.append(scaled.astype(BF16))
    grad_wide = [jnp.concatenate([grad_low[0], zeros], 0), jnp.concatenate([zeros, grad_low[1]], 0)]

    def backward(kb, carry):
        carry = list(carry)
        off = pl.multiple_of(kb * block, block)
        here = pl.ds(off, block)
        v_blk = v_ref[here, :]
        for h in range(2):
            at = slice(h * HEAD, (h + 1) * HEAD)
            e = e_scr[h, here, :]
            ds = (e.astype(F32) * (dot(v_blk, grad_wide[h]) - centre[h])).astype(BF16)
            dv_ref[at, here] += dot(grad_low[h], e, NT)
            dk_ref[at, here] += dot(q_t[at], ds, NT)
            carry[h] = carry[h] + dot(kt[at, here], ds)
        return tuple(carry)

    grads = lax.fori_loop(low, high, backward, (tall, tall))
    turned = [turn(grads[h] * SCALING, cosq_ref[...], -sinq_ref[...]).astype(BF16) for h in range(2)]
    if first:
        dq_ref[...] = jnp.concatenate(turned, 0)
    else:
        off = pl.multiple_of(place * block, block)
        grads_ref[0, :, pl.ds(off, block)] = jnp.concatenate(turned, 0)

        @pl.when(step == pl.num_programs(1) - 1)
        def _():
            other = pl.multiple_of((1 - info_ref[0]) * half, half)
            grads_ref[0, :, pl.ds(other, half)] = dq_in[...]

            def finish(i, _):
                here = pl.ds(pl.multiple_of(i * block, block), block)
                cosine, sine = cos_ref[:, here], -sin_ref[:, here]
                for h in range(2):
                    at = slice(h * HEAD, (h + 1) * HEAD)
                    grads_ref[1, at, here] = turn(dk_ref[at, here], cosine, sine).astype(BF16)
                grads_ref[2, :, here] = dv_ref[:, here].astype(BF16)
                return 0

            lax.fori_loop(0, row_len // block, finish, 0)


def attention(info, group, q_t, k_t, v_t, do_t, k, v, start, cosine, sine, before, base_in=0, after=()):
    base, pairs = group
    width = pairs * PAIR
    row_len = q_t.shape[1]
    half = do_t.shape[1]
    block = 512
    steps = half // block
    first = before is None
    place = lambda p, i, info: (base + p, info[0] * steps + i)
    line = lambda p, i, info: (0, info[0] * steps + i)
    here = pl.BlockSpec((PAIR, block), lambda p, i, info: (p, i))
    wide = pl.BlockSpec((PAIR, row_len), lambda p, i, info: (p, 0))
    of_row = pl.BlockSpec((PAIR, row_len), lambda p, i, info: (base + p, 0))
    here_in = pl.BlockSpec((PAIR, block), lambda p, i, info: (base + p, i))
    tall = pl.BlockSpec((row_len, PAIR), lambda p, i, info: (0, base + p))
    angle = pl.BlockSpec((ROT // 2, block), line)
    args = [info, q_t, k_t, v_t, do_t, k, v, start, cosine, sine]
    specs = [pl.BlockSpec((PAIR, block), place), of_row, of_row, here_in, tall, tall, pl.BlockSpec((1, block), line), angle, angle]
    shape = jax.ShapeDtypeStruct
    scratch = [pltpu.VMEM((2, row_len, block), F32), pltpu.VMEM((2, row_len, block), BF16)]
    if first:
        outs = [shape((width, half), BF16)] * 2 + [shape((width, row_len), F32)] * 2
        out_specs = [here, here, wide, wide]
    else:
        table = pl.BlockSpec((ROT // 2, row_len), lambda p, i, info: (0, 0))
        args += [cosine, sine, *before]
        wide_in = pl.BlockSpec((PAIR, row_len), lambda p, i, info: (base_in + p, 0))
        specs += [table, table, pl.BlockSpec((PAIR, half), lambda p, i, info: (base_in + p, 0)), wide_in, wide_in]
        outs = [shape((width, half), BF16), shape((3, width, row_len), BF16)]
        out_specs = [here, pl.BlockSpec((3, PAIR, row_len), lambda p, i, info: (0, p, 0))]
        scratch += [pltpu.VMEM((PAIR, row_len), F32)] * 2
    args += list(after)
    specs += [pl.BlockSpec(memory_space=pl.ANY)] * len(after)
    return pl.pallas_call(
        functools.partial(attention_body, first=first, block=block, skip=len(after)),
        grid_spec=pltpu.PrefetchScalarGridSpec(
            num_scalar_prefetch=1,
            grid=(pairs, steps),
            in_specs=specs,
            out_specs=out_specs,
            scratch_shapes=scratch,
        ),
        out_shape=outs,
        compiler_params=pltpu.CompilerParams(vmem_limit_bytes=60 * MIB),
        cost_estimate=cost(11 * pairs),
        name="attention",
    )(*args)


def exchange(x, bit):
    return lax.ppermute(x, "dp", [(i, i ^ (1 << bit)) for i in range(lax.axis_size("dp"))])


def orders():
    bits = range(lax.axis_size("dp").bit_length() - 1)
    return [0, *bits[1:]], [0, *bits[2:], 1]


class Sum:
    def __init__(self, x, order):
        self.x = x
        self.stages = [(True, bit) for bit in order] + [(False, bit) for bit in order[::-1]]
        self.sent = None

    def start(self):
        if not self.stages:
            return
        halving, bit = self.stages[0]
        mine = (lax.axis_index("dp") >> bit) & 1
        if halving:
            half = self.x.shape[0] // 2
            self.sent = exchange(lax.dynamic_slice_in_dim(self.x, (1 - mine) * half, half, 0), bit)
        else:
            self.sent = exchange(self.x, bit)

    def finish(self):
        if self.sent is None:
            return
        halving, bit = self.stages.pop(0)
        mine = (lax.axis_index("dp") >> bit) & 1
        if halving:
            half = self.x.shape[0] // 2
            kept = lax.dynamic_slice_in_dim(self.x, mine * half, half, 0)
            self.x = (kept.astype(F32) + self.sent.astype(F32)).astype(BF16)
        else:
            low = jnp.concatenate([self.x, self.sent], 0)
            high = jnp.concatenate([self.sent, self.x], 0)
            self.x = jnp.where(mine == 0, low, high)
        self.sent = None


def tick(*sums):
    for s in sums:
        s.finish()
    arrived = tuple(s.x for s in sums)
    for s in sums:
        s.start()
    return arrived


def small_total(x):
    for bit in orders()[0]:
        x = x + exchange(x, bit)
    return x


def per_device(
    tokens,
    cotangent,
    lengths,
    pad_count,
    ln1_gain,
    ln1_bias,
    ln2_gain,
    ln2_bias,
    qkv_weight,
    qkv_bias,
    out_weight,
    out_bias,
    fc1_weight,
    fc1_bias,
    fc2_weight,
):
    half, d = tokens.shape
    row_len = half * lax.axis_size("mp")
    width = qkv_weight.shape[2]
    hidden = fc1_weight.shape[1]
    me = lax.axis_index("mp")
    swap = [(0, 1), (1, 0)]
    y_first, z_first = orders()
    tok_far = lax.ppermute(tokens, "mp", swap)

    docs = lengths.shape[1]
    order = jnp.arange(docs)
    starts = jnp.sum(jnp.where(order[None, :] < order[:, None], lengths[0][None, :], 0), axis=1)
    places = jnp.arange(row_len, dtype=jnp.int32)
    doc_start = jnp.max(jnp.where(starts[:, None] <= places[None, :], starts[:, None], 0), axis=0)
    kept = row_len - pad_count[0]
    start = jnp.where(places < kept, doc_start, places).astype(jnp.int32)
    frequency = ROTARY_BASE ** (-(jnp.arange(ROT // 2, dtype=F32) * 2.0) / ROT)
    angles = frequency[:, None] * (places - doc_start).astype(F32)[None, :]
    cosine, sine = jnp.cos(angles), jnp.sin(angles)
    block = 512
    lows = (start[::block] // block).astype(jnp.int32).reshape(2, -1)
    near = jnp.concatenate([me[None].astype(jnp.int32), lows[me]])
    far = jnp.concatenate([(1 - me)[None].astype(jnp.int32), lows[1 - me]])
    cot_later, tok_far = lax.optimization_barrier((cotangent, tok_far))
    cot_far = lax.ppermute(cot_later, "mp", swap)
    inside = jnp.arange(half, dtype=jnp.int32)[:, None]
    g_near = jnp.where(inside < kept - me * half, cotangent, jnp.zeros((), BF16))
    g_far = jnp.where(inside < kept - (1 - me) * half, cot_far, jnp.zeros((), BF16))

    gain1, shift1 = ln1_gain[None], ln1_bias[None]
    gain2, shift2 = ln2_gain[None], ln2_bias[None]
    b_col = qkv_bias.reshape(3 * width, 1)
    b1 = fc1_bias[None]

    feed = (gain2, shift2, fc1_weight, b1, fc2_weight)
    wide = hidden // 2
    mlp_near = mlp(tokens, g_near, *feed, wide, 256, (0, 2))
    later, _ = lax.optimization_barrier((qkv_weight, mlp_near[4]))
    w_t = jnp.transpose(later, (1, 2, 0)).reshape(3 * width, d)
    front = (gain1, shift1, w_t, b_col, cosine, sine, row_len)
    made = project(near[:1], tokens, *front, None, (tok_far,))
    q_t, k_t, v_t, k, v, normed1 = project(far[:1], tok_far, *front, made)
    do_near = dot(out_weight, g_near, NT).astype(BF16)
    do_far = dot(out_weight, g_far, NT).astype(BF16)

    def attend(which, group, before, base_in, do_t, after=()):
        return attention(which, group, q_t, k_t, v_t, do_t, k, v, start[None], cosine, sine, before, base_in, after)

    def branch(o, part):
        return dot(o, out_weight, TN) + part.astype(F32)

    every = (0, width // PAIR)
    o_near, *kept_near = attend(near, every, None, 0, do_near)
    mlp_far = mlp(tok_far, g_far, *feed, wide, 256, (0, 2), mlp_near[2:4], None, (o_near,))
    out_far, e2_far = mlp_far[:2]
    grad_fc1, grad_fc2 = lax.psum(mlp_far[2:4], "dp")

    def rest(g_near, g_far, tok_near, tok_far, normed1, w_t, o_near, kept_near, out_near, out_far, e2_near, e2_far, do_far, early, fc1_b):
        o_far, grads = attend(far, every, kept_near, 0, do_far)
        grads = grads.reshape(3 * width, row_len)
        qkv = dot(grads, normed1).astype(BF16)
        out = (dot(o_near, g_near) + dot(o_far, g_far)).astype(BF16)
        arrived = lax.ppermute(branch(o_far, out_far).astype(BF16), "mp", swap)

        def norm_back(place, tok, e2):
            part = lax.dynamic_slice_in_dim(grads, place * half, half, 1)
            back = dot(part, w_t, TN)
            centred, rstd = norm_stats(tok.astype(F32))
            xhat = centred * rstd
            return gain1 * back + e2.astype(F32), jnp.sum(back * xhat, axis=0), jnp.sum(back, axis=0)

        e_far, dgain_far, dshift_far = norm_back(1 - me, tok_far, e2_far)
        e_arrived = lax.ppermute(e_far.astype(BF16), "mp", swap)
        e_near, dgain_near, dshift_near = norm_back(me, tok_near, e2_near)
        late = jnp.stack([dgain_near + dgain_far, dshift_near + dshift_far])
        small = jnp.concatenate([late.reshape(-1), early.reshape(-1), jnp.sum(grads.astype(F32), axis=1), fc1_b])
        small = small_total(small.reshape(-1, 128)).reshape(-1)
        both = small[: 5 * d].reshape(5, d)

        cut = width
        parts = [(out, y_first), (qkv[:cut], z_first), (qkv[cut : 2 * cut], y_first), (qkv[2 * cut :], y_first)]
        parts = [Sum(x, order) for x, order in parts]
        stage = 0
        while any(p.stages for p in parts):
            for p in parts:
                p.finish()
            for p in parts:
                p.start()
            stage += 1

        inputs = tok_near.astype(F32)
        output = (inputs + (branch(o_near, out_near) + arrived.astype(F32)) + out_bias).astype(BF16)
        e = e_near + e_arrived.astype(F32)
        centred, rstd = norm_stats(inputs)
        xhat = centred * rstd
        grad_in = rstd * (e - jnp.mean(e, axis=-1, keepdims=True) - xhat * jnp.mean(e * xhat, axis=-1, keepdims=True))
        grad_tokens = g_near.astype(F32) + grad_in
        both = both + lax.ppermute(both, "mp", swap)
        grad_qkv = jnp.transpose(jnp.stack([p.x for p in parts[1:]]), (2, 0, 1)).astype(F32)
        grad_out_w = parts[0].x.astype(F32)
        return output, grad_tokens, both, small[5 * d :], grad_qkv, grad_out_w

    def never(g_near, g_far, tok_near, *unused):
        zeros = jnp.zeros
        return (
            tok_near,
            zeros((half, d), F32),
            zeros((5, d), F32),
            zeros((3 * width + hidden,), F32),
            zeros((d, 3, width), F32),
            zeros((width, d), F32),
        )

    early = jnp.stack([(mlp_near[5] + mlp_far[5])[0], (mlp_near[6] + mlp_far[6])[0], jnp.sum(lax.optimization_barrier((g_near, mlp_near[4]))[0].astype(F32), axis=0)])
    fc1_b = (mlp_near[4] + mlp_far[4])[0]
    output, grad_tokens, both, small, grad_qkv, grad_out_w = lax.cond(
        jnp.min(lengths) > 0,
        rest,
        never,
        g_near,
        g_far,
        tokens,
        tok_far,
        normed1,
        w_t,
        o_near,
        kept_near,
        mlp_near[0],
        out_far,
        mlp_near[1],
        e2_far,
        do_far,
        early,
        fc1_b,
    )
    grad_qkv_b = small[: 3 * width].reshape(3, width)
    grad_fc1_b = small[3 * width :]
    return (
        output,
        grad_tokens,
        both[0],
        both[1],
        both[2],
        both[3],
        grad_qkv,
        grad_qkv_b,
        grad_out_w,
        both[4],
        grad_fc1.astype(F32),
        grad_fc1_b,
        grad_fc2.astype(F32),
    )


def solution(mesh):
    return jax.shard_map(
        per_device,
        mesh=mesh,
        in_specs=(
            P(("dp", "mp"), None),
            P(("dp", "mp"), None),
            P("dp", None),
            P("dp"),
            P(),
            P(),
            P(),
            P(),
            P(None, None, "mp"),
            P(None, "mp"),
            P("mp", None),
            P(),
            P(None, "mp"),
            P("mp"),
            P("mp", None),
        ),
        out_specs=(
            P(("dp", "mp"), None),
            P(("dp", "mp"), None),
            P(),
            P(),
            P(),
            P(),
            P(None, None, "mp"),
            P(None, "mp"),
            P("mp", None),
            P(),
            P(None, "mp"),
            P("mp"),
            P("mp", None),
        ),
        check_vma=False,
    )
```

```python
import functools

import jax
import jax.numpy as jnp
from jax import lax
from jax.experimental import pallas as pl
from jax.experimental.pallas import tpu as pltpu
from jax.experimental.layout import Layout, with_layout_constraint
from jax.sharding import PartitionSpec as P

HEAD = 64
ROT = 16
PAIR = 2 * HEAD
EPSILON = 1e-05
MASKED_SCORE = -1e30
ROTARY_BASE = 10000.0
SCALING = HEAD**-0.5
F32 = jnp.float32
BF16 = jnp.bfloat16
NN = ((1,), (0,))
NT = ((1,), (1,))
TN = ((0,), (0,))
MIB = 2**20


def dot(a, b, dims=NN):
    return lax.dot_general(a, b, (dims, ((), ())), preferred_element_type=F32)


def cost(micros):
    return pl.CostEstimate(flops=int(micros * 1.1e9), bytes_accessed=0, transcendentals=0)


def norm_stats(v):
    average = jnp.mean(v, axis=-1, keepdims=True)
    centred = v - average
    spread = jnp.mean(centred * centred, axis=-1, keepdims=True)
    return centred, lax.rsqrt(spread + EPSILON)


def turn(x, cosine, sine):
    half = ROT // 2
    u, w = x[:half], x[half:ROT]
    return jnp.concatenate([u * cosine - w * sine, w * cosine + u * sine, x[ROT:]], axis=0)


def project_body(place_ref, tok_ref, gain_ref, shift_ref, w_ref, b_ref, cos_ref, sin_ref, *rest):
    q_out, kt_out, vt_out, k_out, v_out, n_out = rest[-6:]
    x = tok_ref[...].astype(F32)
    centred, rstd = norm_stats(x)
    normed = (centred * rstd * gain_ref[...] + shift_ref[...]).astype(BF16)
    n_out[...] = normed
    cosine, sine = cos_ref[...], sin_ref[...]
    width = k_out.shape[1]

    def head_rows(c, scale):
        p = dot(w_ref[c * width : (c + 1) * width, :], normed, NT) + b_ref[c * width : (c + 1) * width, :]
        if c == 2:
            return p.astype(BF16)
        parts = [turn(p[h : h + HEAD], cosine, sine) for h in range(0, width, HEAD)]
        return (jnp.concatenate(parts, axis=0) * scale).astype(BF16)

    q_out[...] = head_rows(0, SCALING)
    k = head_rows(1, 1.0)
    kt_out[...] = k
    k_out[...] = k.T
    v = head_rows(2, 1.0)
    vt_out[...] = v
    v_out[...] = v.T


def project(place, tok, gain, shift, w_t, b_col, cosine, sine, row_len, before, after=()):
    half, d = tok.shape
    width = w_t.shape[0] // 3
    rows = 256
    steps = half // rows
    here = lambda i, place: (i, 0)
    lanes = lambda i, place: (0, place[0] * steps + i)
    seq = lambda i, place: (place[0] * steps + i, 0)
    fixed = lambda i, place: (0, 0)
    specs = [
        pl.BlockSpec((rows, d), here),
        pl.BlockSpec((1, d), fixed),
        pl.BlockSpec((1, d), fixed),
        pl.BlockSpec((3 * width, d), fixed),
        pl.BlockSpec((3 * width, 1), fixed),
        pl.BlockSpec((ROT // 2, rows), lanes),
        pl.BlockSpec((ROT // 2, rows), lanes),
    ]
    args = [place, tok, gain, shift, w_t, b_col, cosine, sine]
    aliases = {}
    if before is not None:
        specs += [pl.BlockSpec(memory_space=pl.ANY)] * 6
        aliases = {len(args) + i: i for i in range(6)}
        args += list(before)
    args += list(after)
    specs += [pl.BlockSpec(memory_space=pl.ANY)] * len(after)
    wide = jax.ShapeDtypeStruct((width, row_len), BF16)
    tall = jax.ShapeDtypeStruct((row_len, width), BF16)
    return pl.pallas_call(
        project_body,
        grid_spec=pltpu.PrefetchScalarGridSpec(
            num_scalar_prefetch=1,
            grid=(steps,),
            in_specs=specs,
            out_specs=[pl.BlockSpec((width, rows), lanes)] * 3
            + [pl.BlockSpec((rows, width), seq)] * 2
            + [pl.BlockSpec((rows, d), seq)],
        ),
        out_shape=[wide, wide, wide, tall, tall, jax.ShapeDtypeStruct((row_len, d), BF16)],
        input_output_aliases=aliases,
        compiler_params=pltpu.CompilerParams(vmem_limit_bytes=60 * MIB),
        cost_estimate=cost(9),
        name="project",
    )(*args)


def gelu_parts(v):
    t = 1.0 / (1.0 + (0.3275911 * 0.7071067811865476) * jnp.abs(v))
    bell = jnp.exp(-0.5 * (v * v))
    poly = t * (0.127414796 + t * (-0.142248368 + t * (0.7107068705 + t * (-0.7265760135 + t * 0.5307027145))))
    tail = poly * bell
    below = jnp.where(v < 0.0, tail, 1.0 - tail)
    return v * below, below + v * (bell * 0.3989422804014327)


def mlp_body(*refs, first, again, rows, skip):
    tok_ref, g_ref, gain_ref, shift_ref, w1_ref, b1_ref, w2_ref = refs[:7]
    refs = refs[7:]
    if not first:
        dw1_in, dw2_in = refs[:2]
        refs = refs[2:]
    if again:
        out_in, e_in = refs[:2]
        refs = refs[2:]
    refs = refs[skip:]
    out_ref, e_ref, dw1_ref, dw2_ref, db1_ref, dgain_ref, dshift_ref = refs[:7]
    normed, normed_t, out_acc, back_acc, act_t, pre_t = refs[7:]
    step = pl.program_id(0)
    last = pl.num_programs(0) - 1
    half, d = normed.shape
    blocks = half // rows

    @pl.when(step == 0)
    def _():
        def prepare(i, _):
            at = pl.ds(pl.multiple_of(i * rows, rows), rows)
            centred, rstd = norm_stats(tok_ref[at, :].astype(F32))
            n = (centred * rstd * gain_ref[...] + shift_ref[...]).astype(BF16)
            normed[at, :] = n
            normed_t[:, at] = n.T
            return 0

        lax.fori_loop(0, blocks, prepare, 0)
        dgain_ref[...] = jnp.zeros_like(dgain_ref)
        dshift_ref[...] = jnp.zeros_like(dshift_ref)

    def forward(i, bias_sum):
        at = pl.ds(pl.multiple_of(i * rows, rows), rows)
        v = dot(normed[at, :], w1_ref[...]) + b1_ref[...]
        grad_act = dot(g_ref[at, :], w2_ref[...], NT)
        act, slope = gelu_parts(v)
        act = act.astype(BF16)
        grad_pre = (grad_act * slope).astype(BF16)
        out = dot(act, w2_ref[...])
        back = dot(grad_pre, w1_ref[...], NT)

        @pl.when(step == 0)
        def _():
            out_acc[at, :] = out
            back_acc[at, :] = back

        @pl.when(step > 0)
        def _():
            out_acc[at, :] += out
            back_acc[at, :] += back

        act_t[:, at] = act.T
        pre_t[at, :] = grad_pre
        return bias_sum + jnp.sum(grad_pre.astype(F32), axis=0, keepdims=True)

    db1_ref[...] = lax.fori_loop(0, blocks, forward, jnp.zeros(db1_ref.shape, F32))

    def weights(i, _):
        at = pl.ds(pl.multiple_of(i * rows, rows), rows)
        one = dot(normed_t[at, :], pre_t[...])
        if not first:
            one = one + dw1_in[at, :].astype(F32)
        dw1_ref[at, :] = one.astype(BF16)
        two = dot(act_t[...], g_ref[:, at])
        if not first:
            two = two + dw2_in[:, at].astype(F32)
        dw2_ref[:, at] = two.astype(BF16)
        return 0

    for i in range(d // rows):
        weights(i, 0)

    @pl.when(step == last)
    def _():
        def finish(i, _):
            at = pl.ds(pl.multiple_of(i * rows, rows), rows)
            centred, rstd = norm_stats(tok_ref[at, :].astype(F32))
            back = back_acc[at, :]
            dgain_ref[...] += jnp.sum(back * (centred * rstd), axis=0, keepdims=True)
            dshift_ref[...] += jnp.sum(back, axis=0, keepdims=True)
            e, out = back * gain_ref[...], out_acc[at, :]
            if again:
                e, out = e + e_in[at, :].astype(F32), out + out_in[at, :].astype(F32)
            e_ref[at, :] = e.astype(BF16)
            out_ref[at, :] = out.astype(BF16)
            return 0

        lax.fori_loop(0, blocks, finish, 0)


def mlp(tok, g, gain, shift, w1, b1, w2, chunk, rows, span, before=None, partial=None, after=()):
    half, d = tok.shape
    base, chunks = span
    hidden = chunks * chunk
    fixed = lambda j: (0, 0)
    cols = pl.BlockSpec((d, chunk), lambda j: (0, j))
    tall = pl.BlockSpec((chunk, d), lambda j: (j, 0))
    whole = pl.BlockSpec((half, d), fixed)
    line = pl.BlockSpec((1, d), fixed)
    bias = pl.BlockSpec((1, chunk), lambda j: (0, j))
    cols_in = pl.BlockSpec((d, chunk), lambda j: (0, base + j))
    tall_in = pl.BlockSpec((chunk, d), lambda j: (base + j, 0))
    args = [tok, g, gain, shift, w1, b1, w2]
    specs = [whole, whole, line, line, cols_in, pl.BlockSpec((1, chunk), lambda j: (0, base + j)), tall_in]
    if before is not None:
        args += list(before)
        specs += [cols_in, tall_in]
    if partial is not None:
        args += list(partial)
        specs += [whole, whole]
    args += list(after)
    specs += [pl.BlockSpec(memory_space=pl.ANY)] * len(after)
    shape = jax.ShapeDtypeStruct
    return pl.pallas_call(
        functools.partial(mlp_body, first=before is None, again=partial is not None, rows=rows, skip=len(after)),
        grid=(chunks,),
        in_specs=specs,
        out_specs=[whole, whole, cols, tall, bias, line, line],
        out_shape=[
            shape((half, d), BF16),
            shape((half, d), BF16),
            shape((d, hidden), BF16),
            shape((hidden, d), BF16),
            shape((1, hidden), F32),
            shape((1, d), F32),
            shape((1, d), F32),
        ],
        scratch_shapes=[
            pltpu.VMEM((half, d), BF16),
            pltpu.VMEM((d, half), BF16),
            pltpu.VMEM((half, d), F32),
            pltpu.VMEM((half, d), F32),
            pltpu.VMEM((chunk, half), BF16),
            pltpu.VMEM((half, chunk), BF16),
        ],
        compiler_params=pltpu.CompilerParams(vmem_limit_bytes=60 * MIB),
        cost_estimate=cost(44 * hidden / w1.shape[1]),
        name="feed_forward",
    )(*args)


def fold(x, op):
    return op(x.reshape(x.shape[0] // 8, 8, x.shape[1]), axis=0)


def attention_body(info_ref, q_ref, kt, vt, do_ref, k_ref, v_ref, start_ref, cosq_ref, sinq_ref, *rest, first, block, skip):
    if first:
        rest = rest[skip:]
        o_ref, dq_ref, dk_ref, dv_ref, s_scr, e_scr = rest
    else:
        cos_ref, sin_ref, dq_in, dk_in, dv_in = rest[:5]
        o_ref, grads_ref, s_scr, e_scr, dk_ref, dv_ref = rest[5 + skip :]
    step = pl.program_id(1)
    half = pl.num_programs(1) * block
    place = info_ref[0] * pl.num_programs(1) + step
    row_len = kt.shape[1]

    @pl.when(step == 0)
    def _():
        if first:
            dk_ref[...] = jnp.zeros_like(dk_ref)
            dv_ref[...] = jnp.zeros_like(dv_ref)
        else:
            dk_ref[...] = dk_in[...]
            dv_ref[...] = dv_in[...]

    q_t = q_ref[...]
    zeros = jnp.zeros((HEAD, block), BF16)
    q_wide = [jnp.concatenate([q_t[:HEAD], zeros], 0), jnp.concatenate([zeros, q_t[HEAD:]], 0)]
    start = start_ref[...]
    spot = place * block + lax.broadcasted_iota(jnp.int32, (1, block), 1)
    low = info_ref[1 + step]
    high = place + 1
    rows = lax.broadcasted_iota(jnp.int32, (block, block // 2), 0)

    def scores(kb, tops):
        tops = list(tops)
        off = pl.multiple_of(kb * block, block)
        k_blk = k_ref[pl.ds(off, block), :]
        for w in range(2):
            at = slice(w * block // 2, (w + 1) * block // 2)
            legal = (rows >= start[:, at] - off) & (rows <= spot[:, at] - off)
            for h in range(2):
                s = jnp.where(legal, dot(k_blk, q_wide[h][:, at]), MASKED_SCORE)
                s_scr[h, pl.ds(off, block), at] = s
                tops[2 * h + w] = jnp.maximum(tops[2 * h + w], fold(s, jnp.max))
        return tuple(tops)

    tops = lax.fori_loop(low, high, scores, (jnp.full((8, block // 2), MASKED_SCORE, F32),) * 4)
    top = [jnp.max(jnp.concatenate(tops[2 * h : 2 * h + 2], 1), axis=0, keepdims=True) for h in range(2)]

    def forward(kb, carry):
        carry = list(carry)
        off = pl.multiple_of(kb * block, block)
        for h in range(2):
            e = jnp.exp(s_scr[h, pl.ds(off, block), :] - top[h])
            carry[h] = carry[h] + fold(e, jnp.sum)
            e = e.astype(BF16)
            e_scr[h, pl.ds(off, block), :] = e
            carry[2 + h] = carry[2 + h] + dot(vt[h * HEAD : (h + 1) * HEAD, pl.ds(off, block)], e)
        return tuple(carry)

    eight, tall = jnp.zeros((8, block), F32), jnp.zeros((HEAD, block), F32)
    sums = lax.fori_loop(low, high, forward, (eight, eight, tall, tall))
    grad = do_ref[...].astype(F32)
    centre, grad_low, grad_wide = [], [], []
    for h in range(2):
        at = slice(h * HEAD, (h + 1) * HEAD)
        inverse = 1.0 / jnp.sum(sums[h], axis=0, keepdims=True)
        o = sums[2 + h] * inverse
        o_ref[at, :] = o.astype(BF16)
        scaled = grad[at] * inverse
        centre.append(jnp.sum(scaled * o, axis=0, keepdims=True))
        grad_low.append(scaled.astype(BF16))
    grad_wide = [jnp.concatenate([grad_low[0], zeros], 0), jnp.concatenate([zeros, grad_low[1]], 0)]

    def backward(kb, carry):
        carry = list(carry)
        off = pl.multiple_of(kb * block, block)
        here = pl.ds(off, block)
        v_blk = v_ref[here, :]
        for h in range(2):
            at = slice(h * HEAD, (h + 1) * HEAD)
            e = e_scr[h, here, :]
            ds = (e.astype(F32) * (dot(v_blk, grad_wide[h]) - centre[h])).astype(BF16)
            dv_ref[at, here] += dot(grad_low[h], e, NT)
            dk_ref[at, here] += dot(q_t[at], ds, NT)
            carry[h] = carry[h] + dot(kt[at, here], ds)
        return tuple(carry)

    grads = lax.fori_loop(low, high, backward, (tall, tall))
    turned = [turn(grads[h] * SCALING, cosq_ref[...], -sinq_ref[...]).astype(BF16) for h in range(2)]
    if first:
        dq_ref[...] = jnp.concatenate(turned, 0)
    else:
        off = pl.multiple_of(place * block, block)
        grads_ref[0, :, pl.ds(off, block)] = jnp.concatenate(turned, 0)

        @pl.when(step == pl.num_programs(1) - 1)
        def _():
            other = pl.multiple_of((1 - info_ref[0]) * half, half)
            grads_ref[0, :, pl.ds(other, half)] = dq_in[...]

            def finish(i, _):
                here = pl.ds(pl.multiple_of(i * block, block), block)
                cosine, sine = cos_ref[:, here], -sin_ref[:, here]
                for h in range(2):
                    at = slice(h * HEAD, (h + 1) * HEAD)
                    grads_ref[1, at, here] = turn(dk_ref[at, here], cosine, sine).astype(BF16)
                grads_ref[2, :, here] = dv_ref[:, here].astype(BF16)
                return 0

            lax.fori_loop(0, row_len // block, finish, 0)


def attention(info, group, q_t, k_t, v_t, do_t, k, v, start, cosine, sine, before, base_in=0, after=()):
    base, pairs = group
    width = pairs * PAIR
    row_len = q_t.shape[1]
    half = do_t.shape[1]
    block = 512
    steps = half // block
    first = before is None
    place = lambda p, i, info: (base + p, info[0] * steps + i)
    line = lambda p, i, info: (0, info[0] * steps + i)
    here = pl.BlockSpec((PAIR, block), lambda p, i, info: (p, i))
    wide = pl.BlockSpec((PAIR, row_len), lambda p, i, info: (p, 0))
    of_row = pl.BlockSpec((PAIR, row_len), lambda p, i, info: (base + p, 0))
    here_in = pl.BlockSpec((PAIR, block), lambda p, i, info: (base + p, i))
    tall = pl.BlockSpec((row_len, PAIR), lambda p, i, info: (0, base + p))
    angle = pl.BlockSpec((ROT // 2, block), line)
    args = [info, q_t, k_t, v_t, do_t, k, v, start, cosine, sine]
    specs = [pl.BlockSpec((PAIR, block), place), of_row, of_row, here_in, tall, tall, pl.BlockSpec((1, block), line), angle, angle]
    shape = jax.ShapeDtypeStruct
    scratch = [pltpu.VMEM((2, row_len, block), F32), pltpu.VMEM((2, row_len, block), BF16)]
    if first:
        outs = [shape((width, half), BF16)] * 2 + [shape((width, row_len), F32)] * 2
        out_specs = [here, here, wide, wide]
    else:
        table = pl.BlockSpec((ROT // 2, row_len), lambda p, i, info: (0, 0))
        args += [cosine, sine, *before]
        wide_in = pl.BlockSpec((PAIR, row_len), lambda p, i, info: (base_in + p, 0))
        specs += [table, table, pl.BlockSpec((PAIR, half), lambda p, i, info: (base_in + p, 0)), wide_in, wide_in]
        outs = [shape((width, half), BF16), shape((3, width, row_len), BF16)]
        out_specs = [here, pl.BlockSpec((3, PAIR, row_len), lambda p, i, info: (0, p, 0))]
        scratch += [pltpu.VMEM((PAIR, row_len), F32)] * 2
    args += list(after)
    specs += [pl.BlockSpec(memory_space=pl.ANY)] * len(after)
    return pl.pallas_call(
        functools.partial(attention_body, first=first, block=block, skip=len(after)),
        grid_spec=pltpu.PrefetchScalarGridSpec(
            num_scalar_prefetch=1,
            grid=(pairs, steps),
            in_specs=specs,
            out_specs=out_specs,
            scratch_shapes=scratch,
        ),
        out_shape=outs,
        compiler_params=pltpu.CompilerParams(vmem_limit_bytes=60 * MIB),
        cost_estimate=cost(11 * pairs),
        name="attention",
    )(*args)


def exchange(x, bit):
    return lax.ppermute(x, "dp", [(i, i ^ (1 << bit)) for i in range(lax.axis_size("dp"))])


def orders():
    bits = range(lax.axis_size("dp").bit_length() - 1)
    return [0, *bits[1:]], [0, *bits[2:], 1]


class Sum:
    def __init__(self, x, order):
        self.x = x
        self.stages = [(True, bit) for bit in order] + [(False, bit) for bit in order[::-1]]
        self.sent = None

    def start(self):
        if not self.stages:
            return
        halving, bit = self.stages[0]
        mine = (lax.axis_index("dp") >> bit) & 1
        if halving:
            half = self.x.shape[0] // 2
            self.sent = exchange(lax.dynamic_slice_in_dim(self.x, (1 - mine) * half, half, 0), bit)
        else:
            self.sent = exchange(self.x, bit)

    def finish(self):
        if self.sent is None:
            return
        halving, bit = self.stages.pop(0)
        mine = (lax.axis_index("dp") >> bit) & 1
        if halving:
            half = self.x.shape[0] // 2
            kept = lax.dynamic_slice_in_dim(self.x, mine * half, half, 0)
            self.x = (kept.astype(F32) + self.sent.astype(F32)).astype(BF16)
        else:
            low = jnp.concatenate([self.x, self.sent], 0)
            high = jnp.concatenate([self.sent, self.x], 0)
            self.x = jnp.where(mine == 0, low, high)
        self.sent = None


def tick(*sums):
    for s in sums:
        s.finish()
    arrived = tuple(s.x for s in sums)
    for s in sums:
        s.start()
    return arrived


def small_total(x):
    for bit in orders()[0]:
        x = x + exchange(x, bit)
    return x


def per_device(
    tokens,
    cotangent,
    lengths,
    pad_count,
    ln1_gain,
    ln1_bias,
    ln2_gain,
    ln2_bias,
    qkv_weight,
    qkv_bias,
    out_weight,
    out_bias,
    fc1_weight,
    fc1_bias,
    fc2_weight,
):
    half, d = tokens.shape
    row_len = half * lax.axis_size("mp")
    width = qkv_weight.shape[2]
    hidden = fc1_weight.shape[1]
    me = lax.axis_index("mp")
    swap = [(0, 1), (1, 0)]
    y_first, z_first = orders()
    tok_far = lax.ppermute(tokens, "mp", swap)

    docs = lengths.shape[1]
    order = jnp.arange(docs)
    starts = jnp.sum(jnp.where(order[None, :] < order[:, None], lengths[0][None, :], 0), axis=1)
    places = jnp.arange(row_len, dtype=jnp.int32)
    doc_start = jnp.max(jnp.where(starts[:, None] <= places[None, :], starts[:, None], 0), axis=0)
    kept = row_len - pad_count[0]
    start = jnp.where(places < kept, doc_start, places).astype(jnp.int32)
    frequency = ROTARY_BASE ** (-(jnp.arange(ROT // 2, dtype=F32) * 2.0) / ROT)
    angles = frequency[:, None] * (places - doc_start).astype(F32)[None, :]
    cosine, sine = jnp.cos(angles), jnp.sin(angles)
    block = 512
    lows = (start[::block] // block).astype(jnp.int32).reshape(2, -1)
    near = jnp.concatenate([me[None].astype(jnp.int32), lows[me]])
    far = jnp.concatenate([(1 - me)[None].astype(jnp.int32), lows[1 - me]])
    cot_later, tok_far = lax.optimization_barrier((cotangent, tok_far))
    cot_far = lax.ppermute(cot_later, "mp", swap)
    inside = jnp.arange(half, dtype=jnp.int32)[:, None]
    g_near = jnp.where(inside < kept - me * half, cotangent, jnp.zeros((), BF16))
    g_far = jnp.where(inside < kept - (1 - me) * half, cot_far, jnp.zeros((), BF16))

    gain1, shift1 = ln1_gain[None], ln1_bias[None]
    gain2, shift2 = ln2_gain[None], ln2_bias[None]
    b_col = qkv_bias.reshape(3 * width, 1)
    b1 = fc1_bias[None]

    feed = (gain2, shift2, fc1_weight, b1, fc2_weight)
    wide = hidden // 2
    mlp_near = mlp(tokens, g_near, *feed, wide, 256, (0, 2))
    later, _ = lax.optimization_barrier((qkv_weight, mlp_near[4]))
    w_t = jnp.transpose(later, (1, 2, 0)).reshape(3 * width, d)
    front = (gain1, shift1, w_t, b_col, cosine, sine, row_len)
    made = project(near[:1], tokens, *front, None, (tok_far,))
    q_t, k_t, v_t, k, v, normed1 = project(far[:1], tok_far, *front, made)
    do_near = dot(out_weight, g_near, NT).astype(BF16)
    do_far = dot(out_weight, g_far, NT).astype(BF16)

    def attend(which, group, before, base_in, do_t, after=()):
        return attention(which, group, q_t, k_t, v_t, do_t, k, v, start[None], cosine, sine, before, base_in, after)

    def branch(o, part):
        return dot(o, out_weight, TN) + part.astype(F32)

    every = (0, width // PAIR)
    o_near, *kept_near = attend(near, every, None, 0, do_near)
    mlp_far = mlp(tok_far, g_far, *feed, wide, 256, (0, 2), mlp_near[2:4], None, (o_near,))
    out_far, e2_far = mlp_far[:2]
    grad_fc1, grad_fc2 = lax.psum(mlp_far[2:4], "dp")

    def rest(g_near, g_far, tok_near, tok_far, normed1, w_t, o_near, kept_near, out_near, out_far, e2_near, e2_far, do_far, early, fc1_b):
        o_far, grads = attend(far, every, kept_near, 0, do_far)
        qkv = [dot(normed1, grads[c], ((0,), (1,))).astype(BF16) for c in range(3)]
        qkv = [with_layout_constraint(x, Layout(major_to_minor=(0, 1))) for x in qkv]
        grads = grads.reshape(3 * width, row_len)
        out = (dot(o_near, g_near) + dot(o_far, g_far)).astype(BF16)
        arrived = lax.ppermute(branch(o_far, out_far).astype(BF16), "mp", swap)

        def norm_back(place, tok, e2):
            part = lax.dynamic_slice_in_dim(grads, place * half, half, 1)
            back = dot(part, w_t, TN)
            centred, rstd = norm_stats(tok.astype(F32))
            xhat = centred * rstd
            return gain1 * back + e2.astype(F32), jnp.sum(back * xhat, axis=0), jnp.sum(back, axis=0)

        e_far, dgain_far, dshift_far = norm_back(1 - me, tok_far, e2_far)
        e_arrived = lax.ppermute(e_far.astype(BF16), "mp", swap)
        e_near, dgain_near, dshift_near = norm_back(me, tok_near, e2_near)
        late = jnp.stack([dgain_near + dgain_far, dshift_near + dshift_far])
        small = jnp.concatenate([late.reshape(-1), early.reshape(-1), jnp.sum(grads.astype(F32), axis=1), fc1_b])
        small = small_total(small.reshape(-1, 128)).reshape(-1)
        both = small[: 5 * d].reshape(5, d)

        parts = [(out, y_first), (qkv[0], z_first), (qkv[1], y_first), (qkv[2], y_first)]
        parts = [Sum(x, order) for x, order in parts]
        stage = 0
        while any(p.stages for p in parts):
            for p in parts:
                p.finish()
            for p in parts:
                p.start()
            stage += 1

        inputs = tok_near.astype(F32)
        output = (inputs + (branch(o_near, out_near) + arrived.astype(F32)) + out_bias).astype(BF16)
        e = e_near + e_arrived.astype(F32)
        centred, rstd = norm_stats(inputs)
        xhat = centred * rstd
        grad_in = rstd * (e - jnp.mean(e, axis=-1, keepdims=True) - xhat * jnp.mean(e * xhat, axis=-1, keepdims=True))
        grad_tokens = g_near.astype(F32) + grad_in
        both = both + lax.ppermute(both, "mp", swap)
        grad_qkv = jnp.transpose(jnp.stack([p.x.astype(F32) for p in parts[1:]]), (1, 0, 2))
        grad_out_w = parts[0].x.astype(F32)
        return output, grad_tokens, both, small[5 * d :], grad_qkv, grad_out_w

    def never(g_near, g_far, tok_near, *unused):
        zeros = jnp.zeros
        return (
            tok_near,
            zeros((half, d), F32),
            zeros((5, d), F32),
            zeros((3 * width + hidden,), F32),
            zeros((d, 3, width), F32),
            zeros((width, d), F32),
        )

    early = jnp.stack([(mlp_near[5] + mlp_far[5])[0], (mlp_near[6] + mlp_far[6])[0], jnp.sum(lax.optimization_barrier((g_near, mlp_near[4]))[0].astype(F32), axis=0)])
    fc1_b = (mlp_near[4] + mlp_far[4])[0]
    output, grad_tokens, both, small, grad_qkv, grad_out_w = lax.cond(
        jnp.min(lengths) > 0,
        rest,
        never,
        g_near,
        g_far,
        tokens,
        tok_far,
        normed1,
        w_t,
        o_near,
        kept_near,
        mlp_near[0],
        out_far,
        mlp_near[1],
        e2_far,
        do_far,
        early,
        fc1_b,
    )
    grad_qkv_b = small[: 3 * width].reshape(3, width)
    grad_fc1_b = small[3 * width :]
    return (
        output,
        grad_tokens,
        both[0],
        both[1],
        both[2],
        both[3],
        grad_qkv,
        grad_qkv_b,
        grad_out_w,
        both[4],
        grad_fc1.astype(F32),
        grad_fc1_b,
        grad_fc2.astype(F32),
    )


def solution(mesh):
    return jax.shard_map(
        per_device,
        mesh=mesh,
        in_specs=(
            P(("dp", "mp"), None),
            P(("dp", "mp"), None),
            P("dp", None),
            P("dp"),
            P(),
            P(),
            P(),
            P(),
            P(None, None, "mp"),
            P(None, "mp"),
            P("mp", None),
            P(),
            P(None, "mp"),
            P("mp"),
            P("mp", None),
        ),
        out_specs=(
            P(("dp", "mp"), None),
            P(("dp", "mp"), None),
            P(),
            P(),
            P(),
            P(),
            P(None, None, "mp"),
            P(None, "mp"),
            P("mp", None),
            P(),
            P(None, "mp"),
            P("mp"),
            P("mp", None),
        ),
        check_vma=False,
    )
```
